128 devices in a mesh: sector: 32 (over y, x, z_lo), blk: 4 (over z_hi, core).
Axes of the slice: x: 4, y: 4, z: 4 (z_hi: 2, z_lo: 2; z = z_hi * 2 + z_lo), core: 2. Of those that a mesh axis runs over, the one named last changes fastest.
Arguments:
- features: bfloat16 [512, 64, 2048], P('sector', 'blk'), may hold values from -6 to 6
- residual_first: bfloat16 [3, 3, 64, 64], replicated, may hold values from -0.25 to 0.25
- residual_second: bfloat16 [3, 3, 64, 64], replicated, may hold values from -0.25 to 0.25
- shortcut_first: bfloat16 [3, 3, 64, 64], replicated, may hold values from -0.25 to 0.25
- shortcut_second: bfloat16 [3, 3, 64, 64], replicated, may hold values from -0.25 to 0.25
- first_reduce_weight: bfloat16 [3, 3, 3, 64, 128], replicated, may hold values from -0.15625 to 0.15625
- second_reduce_weight: bfloat16 [3, 3, 3, 128, 256], replicated, may hold values from -0.109375 to 0.109375
- coarse_kernel: bfloat16 [3, 3, 3, 256, 256], P(None, None, None, None, 'blk'), may hold values from -0.078125 to 0.078125
Outputs:
- coarse: bfloat16 [128, 16, 2048], P('sector', None, 'blk')
The draws below stay inside these ranges and needn't reach their ends.
All inputs are finite; a program needn't handle non-finite values.
Results may differ from the reference program's by a relative error of at most 0.009.
Values may be sent and summed in bfloat16 or wider, within the bound.
No kernel may reach another device: no remote copies, remote signals or barrier semaphores. Data moves between devices by JAX's collectives and lax.ppermute only.
A program may use at most 128 MiB of HBM per device.

```python
import jax
import jax.numpy as jnp
from jax import lax

C0 = 64
C1 = 128
C2 = 256
AZ_DEV = 16
HGT = 32
NA = 512
NR = 64
NA4 = 128
NR4 = 16
H4 = 8
N_SECTOR = 32


def level_of(own_key, extent, pieces, least, top_value):
    level, own = 1.0, jax.random.fold_in(own_key, 6)
    for position, parts in pieces:
        steps = jnp.exp(jax.random.uniform(jax.random.fold_in(own, position), (parts,), jnp.float32, least / len(pieces), top_value / len(pieces)))
        level = level * jnp.repeat(steps, extent[position] // parts).reshape([-1 if axis == position else 1 for axis in range(len(extent))])
    return level


def centred(rng, dims, deviation, most, cuts=(), kind=jnp.bfloat16):
    gain = level_of(rng, dims, cuts, -0.22, 0.18) if cuts else 1.0
    entries = jax.random.normal(rng, dims, jnp.float32) * deviation * gain
    return jnp.minimum(jnp.maximum(entries, -most), most).astype(kind)


def setup_inputs(seed: int = 0) -> dict:
    keys = jax.random.split(jax.random.key(seed), 9)
    features = centred(keys[0], (NA, NR, HGT * C0), 1.0, 6.0, ((0, 32), (1, 4)))
    residual_first = centred(keys[1], (3, 3, C0, C0), (9 * C0) ** -0.5, 0.25)
    residual_second = centred(keys[2], (3, 3, C0, C0), (9 * C0) ** -0.5, 0.25)
    shortcut_first = centred(keys[3], (3, 3, C0, C0), (9 * C0) ** -0.5, 0.25)
    shortcut_second = centred(keys[4], (3, 3, C0, C0), (9 * C0) ** -0.5, 0.25)
    first_reduce_weight = centred(keys[5], (3, 3, 3, C0, C1), (27 * C0) ** -0.5, 0.15625)
    second_reduce_weight = centred(keys[6], (3, 3, 3, C1, C2), (27 * C1) ** -0.5, 0.109375)
    coarse_kernel = centred(keys[7], (3, 3, 3, C2, C2), (27 * C2) ** -0.5, 0.078125, ((4, 4),))
    return dict(features=features, residual_first=residual_first, residual_second=residual_second, shortcut_first=shortcut_first, shortcut_second=shortcut_second, first_reduce_weight=first_reduce_weight, second_reduce_weight=second_reduce_weight, coarse_kernel=coarse_kernel)


def leaky_relu(values):
    return jnp.where(values > 0, values, 0.01 * values)


def convolve(source, filter_weight, strides, padding):
    result = lax.conv_general_dilated(source[None], filter_weight.astype(jnp.float32), strides, padding, dimension_numbers=("NDHWC", "DHWIO", "NDHWC"), precision=lax.Precision.HIGHEST)
    return result[0]


def merge_blocks(blocks):
    return blocks.reshape((blocks.shape[0] * blocks.shape[1],) + blocks.shape[2:])


def reference(features, residual_first, residual_second, shortcut_first, shortcut_second, first_reduce_weight, second_reduce_weight, coarse_kernel):
    grid = features.reshape(NA, NR, HGT, C0)

    def context_rows(index):
        row_ids = (index * AZ_DEV - 1 + jnp.arange(AZ_DEV + 2, dtype=jnp.int32)) % NA
        source = jnp.take(grid, row_ids, axis=0).astype(jnp.float32)
        first_res = leaky_relu(convolve(source, residual_first[:, None], (1, 1, 1), ((0, 0), (0, 0), (1, 1)))).astype(jnp.bfloat16)
        res_part = leaky_relu(convolve(first_res.astype(jnp.float32), residual_second[None], (1, 1, 1), ((0, 0), (1, 1), (1, 1))))
        first_short = leaky_relu(convolve(source, shortcut_first[None], (1, 1, 1), ((0, 0), (1, 1), (1, 1)))).astype(jnp.bfloat16)
        short_part = leaky_relu(convolve(first_short.astype(jnp.float32), shortcut_second[:, None], (1, 1, 1), ((0, 0), (0, 0), (1, 1))))
        return (res_part + short_part).astype(jnp.bfloat16)

    finer_features = merge_blocks(lax.map(context_rows, jnp.arange(N_SECTOR, dtype=jnp.int32)))

    def down_level(level, filter_weight, count):
        total_rows = level.shape[0]

        def one_block(index):
            row_ids = (index * 2 * count - 1 + jnp.arange(2 * count + 1, dtype=jnp.int32)) % total_rows
            source = jnp.take(level, row_ids, axis=0).astype(jnp.float32)
            return leaky_relu(convolve(source, filter_weight, (2, 2, 2), ((0, 0), (1, 0), (1, 0)))).astype(jnp.bfloat16)

        return merge_blocks(lax.map(one_block, jnp.arange(total_rows // (2 * count), dtype=jnp.int32)))

    halved_features = down_level(finer_features, first_reduce_weight, AZ_DEV // 2)
    quartered_features = down_level(halved_features, second_reduce_weight, AZ_DEV // 4)
    count = AZ_DEV // 4

    def coarse_rows(index):
        row_ids = (index * count - 1 + jnp.arange(count + 2, dtype=jnp.int32)) % NA4
        source = jnp.take(quartered_features, row_ids, axis=0).astype(jnp.float32)
        summed = convolve(source, coarse_kernel, (1, 1, 1), ((0, 0), (1, 1), (1, 1)))
        result = (source[1:count + 1] + leaky_relu(summed)).astype(jnp.bfloat16)
        return jnp.transpose(result, (0, 1, 3, 2)).reshape(count, NR4, C2 * H4)

    return merge_blocks(lax.map(coarse_rows, jnp.arange(NA4 // count, dtype=jnp.int32)))
```

```python
import jax
import jax.numpy as jnp
from jax import lax
from jax.experimental import pallas as pl
from jax.experimental.pallas import tpu as pltpu
from jax.sharding import PartitionSpec as P

BF = jnp.bfloat16
F32 = jnp.float32
EDGE = 5
VMEM = pl.BlockSpec(memory_space=pltpu.VMEM)


def leaky_relu(values):
    return jnp.maximum(values, 0.01 * values)


def beside(tiles):
    gap = jnp.zeros(tiles.shape[:-2] + (1, tiles.shape[-1]), tiles.dtype)
    after = jnp.concatenate([tiles[..., 1:, :], gap], axis=-2)
    before = jnp.concatenate([gap, tiles[..., :-1, :]], axis=-2)
    lane = lax.broadcasted_iota(jnp.int32, tiles.shape, tiles.ndim - 1)
    return jnp.where(lane < 64, after, before)


def put(ref, index, tiles):
    ref[index + (slice(None), slice(0, 128))] = tiles
    ref[index + (slice(None), slice(128, 256))] = beside(tiles)


def flat(tiles):
    return tiles.reshape(-1, tiles.shape[-1])


def pair_dot(source, weights, slots):
    total = None
    for slot in range(4):
        term = jnp.dot(flat(source(slot)), weights[slot], preferred_element_type=F32)
        total = term if total is None else total + term
    return leaky_relu(total)


def tiles_kernel(x_ref, tiles_ref, sector_ref, band_ref, corner_ref):
    for a in range(x_ref.shape[0]):
        tiles = x_ref[a].reshape(x_ref.shape[1], 16, 128)
        tiles_ref[a] = tiles
        band_ref[a] = tiles[:EDGE]
        if a < EDGE:
            sector_ref[a] = tiles
            corner_ref[a] = tiles[:EDGE]


def weights_kernel(*refs):
    convs, first_ref, coarse_ref = refs[:4], refs[4], refs[5]
    conv_outs, first_out, coarse_out, spread_out = refs[6:10], refs[10], refs[11], refs[12]
    zero = jnp.zeros((64, 64), BF)
    heights = (0, 1, 2, -1)
    for ref, out in zip(convs, conv_outs):
        for slot in range(4):
            for block, height in enumerate(heights):
                for side in range(2):
                    tap = slot - side
                    parts = []
                    for own in range(2):
                        k = height - own + 1
                        inside = 0 <= tap <= 2 and 0 <= k <= 2
                        parts.append(ref[tap, k] if inside else zero)
                    out[slot, 64 * block : 64 * block + 64, 128 * side : 128 * side + 128] = (
                        jnp.concatenate(parts, axis=1)
                    )
    for i in range(3):
        for j in range(3):
            first_out[i, j, 0:64] = first_ref[i, j, 1]
            first_out[i, j, 64:128] = first_ref[i, j, 2]
            first_out[i, j, 128:192] = jnp.zeros((64, 128), BF)
            first_out[i, j, 192:256] = first_ref[i, j, 0]
    band = lax.axis_index("blk")
    row = lax.broadcasted_iota(jnp.int32, (256, 64), 0)
    col = lax.broadcasted_iota(jnp.int32, (256, 64), 1)
    own = jnp.where(row == col + 64 * band, 1.0, 0.0).astype(BF)
    none = jnp.zeros((256, 64), BF)
    for i in range(3):
        for k in range(3):
            last = own if i == 1 and k == 1 else none
            cols = [coarse_ref[i, 0, k], coarse_ref[i, 1, k], coarse_ref[i, 2, k], last]
            coarse_out[i, k] = jnp.concatenate(cols, axis=1)
    row = lax.broadcasted_iota(jnp.int32, (64, 512), 0)
    col = lax.broadcasted_iota(jnp.int32, (64, 512), 1)
    for h in range(8):
        spread_out[h] = jnp.where(col == row * 8 + h, 1.0, 0.0).astype(BF)


def down_kernel(
    tiles_ref, sector_ref, band_ref, corner_ref,
    wp_ref, wp2_ref, wq_ref, wq2_ref, w1_ref, w2_ref,
    y_ref, xx, pp, qq, ff, part, gg,
):
    own = tiles_ref.shape[0]
    blank = jnp.zeros((1, 16, 256), BF)
    for a in range(22):
        xx[a, 0:1] = blank
    xx[0] = jnp.zeros((22, 16, 256), BF)
    for a in range(own):
        put(xx, (a + 1, slice(1, own + 1)), tiles_ref[a])
        put(xx, (a + 1, slice(own + 1, own + 1 + EDGE)), band_ref[a])
    for a in range(EDGE):
        put(xx, (own + a + 1, slice(1, own + 1)), sector_ref[a])
        put(xx, (own + a + 1, slice(own + 1, own + 1 + EDGE)), corner_ref[a])
    for a in range(20):
        pp[a, 0:1] = blank
    for pair in range(10):
        total = pair_dot(lambda s: xx[2 * pair + s, 1:22], wp_ref, 4)
        for side in range(2):
            tiles = total[:, 128 * side : 128 * side + 128].astype(BF).reshape(21, 16, 128)
            put(pp, (2 * pair + side, slice(1, 22)), tiles)
    qq[0] = jnp.zeros((20, 16, 256), BF)
    for pair in range(10):
        total = pair_dot(lambda s: xx[1:22, 2 * pair + s], wq_ref, 4)
        for side in range(2):
            tiles = total[:, 128 * side : 128 * side + 128].astype(BF).reshape(21, 16, 128)
            put(qq, (slice(1, 22), 2 * pair + side), tiles)
    for pair in range(10):
        total = pair_dot(lambda s: pp[0:20, 2 * pair + s], wp2_ref, 4)
        for side in range(2):
            part[:, 2 * pair + side] = total[:, 128 * side : 128 * side + 128].reshape(20, 16, 128)
    for a in range(20):
        ff[a, 0:1] = blank
    for pair in range(10):
        total = pair_dot(lambda s: qq[2 * pair + s], wq2_ref, 4)
        for side in range(2):
            a = 2 * pair + side
            tiles = total[:, 128 * side : 128 * side + 128].reshape(20, 16, 128)
            put(ff, (a, slice(1, 21)), (part[a] + tiles).astype(BF))
    for a in range(9):
        gg[a, 0:1] = jnp.zeros((1, 16, 128), F32)
    for a in range(9):
        total = None
        for i in range(3):
            for j in range(3):
                rows = jnp.stack([ff[2 * a + 1 + i, j + 2 * r] for r in range(10)])
                term = jnp.dot(flat(rows), w1_ref[i, j], preferred_element_type=F32)
                total = term if total is None else total + term
        total = leaky_relu(total).astype(BF).astype(F32)
        gg[a, 1:11] = total.reshape(10, 16, 128)
    gap = jnp.zeros((1, 128), F32)
    cells = {}
    for a in range(9):
        for r in range(11):
            even = gg[a, r, pl.ds(0, 8, stride=2), :]
            odd = gg[a, r, pl.ds(1, 8, stride=2), :]
            under = jnp.concatenate([gap, odd[:-1]], axis=0)
            cells[a, r] = jnp.concatenate([even, odd, under], axis=1)
    total = None
    for i in range(3):
        for j in range(3):
            rows = jnp.concatenate([cells[2 * a + i, 2 * r + j] for a in range(4) for r in range(5)], axis=0).astype(BF)
            term = jnp.dot(rows[:, 0:256], w2_ref[i, j, 1:3].reshape(256, 256), preferred_element_type=F32)
            term = term + jnp.dot(rows[:, 256:384], w2_ref[i, j, 0], preferred_element_type=F32)
            total = term if total is None else total + term
    y_ref[...] = leaky_relu(total).astype(BF)


def coarse_kernel_body(own_ref, near_ref, far_ref, wc_ref, spread_ref, out_ref, slab, moved):
    band = lax.axis_index("blk")
    for place, ref, index in ((0, own_ref, None), (1, near_ref, None), (2, far_ref, 0), (3, far_ref, 1)):
        other = jnp.bitwise_xor(band, place)
        block = (ref[...] if index is None else ref[index]).astype(F32).reshape(6, 5, 8, 256)
        slab[:, pl.ds(4 * other + 1, 4)] = block[:, 1:5]

        @pl.when(other == 0)
        def _():
            slab[:, 0:1] = block[:, 0:1]

    for a in range(4):
        rows = [slab[a + i, 0:16].astype(BF).reshape(128, 256) for i in range(3)]
        tall = None
        for k in range(3):
            total = None
            for i in range(3):
                term = jnp.dot(rows[i], wc_ref[i, k], preferred_element_type=F32)
                total = term if total is None else total + term
            total = total.reshape(16, 8, 256)
            gap = jnp.zeros((16, 1, 256), F32)
            if k == 0:
                total = jnp.concatenate([gap, total[:, :-1]], axis=1)
            elif k == 2:
                total = jnp.concatenate([total[:, 1:], gap], axis=1)
            else:
                kept = total[:, :, 192:256]
            tall = total if tall is None else tall + total
        gap = jnp.zeros((1, 8, 64), F32)
        total = (
            jnp.concatenate([gap, tall[:-1, :, 0:64]], axis=0)
            + tall[:, :, 64:128]
            + jnp.concatenate([tall[1:, :, 128:192], gap], axis=0)
        )
        moved[128 * a : 128 * a + 128, 0:64] = (kept + leaky_relu(total)).reshape(128, 64)
    total = None
    for h in range(8):
        rows = moved[pl.ds(h, 64, stride=8), :].astype(BF)
        term = jnp.dot(rows[:, 0:64], spread_ref[h], preferred_element_type=F32)
        total = term if total is None else total + term
    out_ref[...] = total.astype(BF).reshape(4, 16, 512)


def moved_by(x, sectors, band_of):
    count, bands = lax.axis_size("sector"), lax.axis_size("blk")
    pairs = []
    for s in range(count):
        for b in range(bands):
            if 0 <= band_of(b) < bands:
                pairs.append((s * bands + b, (s + sectors) % count * bands + band_of(b)))
    return lax.ppermute(x, ("sector", "blk"), pairs)


def shaped(*dims, dtype=BF):
    return jax.ShapeDtypeStruct(dims, dtype)


def run(kernel, outs, scratch, flops, name, *args):
    return pl.pallas_call(
        kernel,
        out_shape=outs,
        in_specs=[VMEM] * len(args),
        out_specs=jax.tree.map(lambda _: VMEM, outs),
        scratch_shapes=scratch,
        compiler_params=pltpu.CompilerParams(vmem_limit_bytes=40 << 20),
        cost_estimate=pl.CostEstimate(flops=flops, bytes_accessed=1 << 20, transcendentals=0),
        name=name,
    )(*args)


def per_device(features, residual_first, residual_second, shortcut_first, shortcut_second,
               first_reduce_weight, second_reduce_weight, coarse_kernel):
    tiles, sector_edge, band_edge, corner = run(
        tiles_kernel,
        (shaped(16, 16, 16, 128), shaped(EDGE, 16, 16, 128), shaped(16, EDGE, 16, 128), shaped(EDGE, EDGE, 16, 128)),
        (), 1 << 30, "tiles", features,
    )
    sector_edge = moved_by(sector_edge, -1, lambda b: b)
    band_edge = moved_by(band_edge, 0, lambda b: b - 1)
    corner = moved_by(corner, -1, lambda b: b - 1)
    *convs, w1, wc, spread = run(
        weights_kernel,
        (shaped(4, 256, 256),) * 4 + (shaped(3, 3, 256, 128), shaped(3, 3, 256, 256), shaped(8, 64, 512)),
        (), 1 << 30, "weights",
        residual_first, residual_second, shortcut_first, shortcut_second, first_reduce_weight, coarse_kernel,
    )
    y = run(
        down_kernel,
        shaped(160, 256),
        (
            pltpu.VMEM((22, 22, 16, 256), BF),
            pltpu.VMEM((20, 22, 16, 256), BF),
            pltpu.VMEM((22, 20, 16, 256), BF),
            pltpu.VMEM((20, 21, 16, 256), BF),
            pltpu.VMEM((20, 20, 16, 128), F32),
            pltpu.VMEM((9, 11, 16, 128), F32),
        ),
        10 << 30, "down", tiles, sector_edge, band_edge, corner, *convs, w1, second_reduce_weight,
    )
    y = jnp.concatenate([moved_by(y[80:160], 1, lambda b: b), y], axis=0)
    far = moved_by(y, 0, lambda b: b ^ 2)
    both = jnp.stack([y, far])
    other = moved_by(both, 0, lambda b: b ^ 1)
    return run(
        coarse_kernel_body,
        shaped(4, 16, 512),
        (pltpu.VMEM((6, 18, 8, 256), F32), pltpu.VMEM((512, 128), F32)),
        2 << 30, "coarse", y, other[0], jnp.stack([far, other[1]]), wc, spread,
    )


def solution(mesh):
    in_specs = (P("sector", "blk", None),) + (P(),) * 6 + (P(None, None, None, None, "blk"),)
    return jax.shard_map(
        per_device, mesh=mesh, in_specs=in_specs, out_specs=P("sector", None, "blk"), check_vma=False
    )
```

```python
import jax
import jax.numpy as jnp
from jax import lax
from jax.experimental import pallas as pl
from jax.experimental.pallas import tpu as pltpu
from jax.sharding import PartitionSpec as P

BF = jnp.bfloat16
F32 = jnp.float32
EDGE = 5
VMEM = pl.BlockSpec(memory_space=pltpu.VMEM)


def leaky_relu(values):
    return jnp.maximum(values, 0.01 * values)


def beside(tiles):
    gap = jnp.zeros(tiles.shape[:-2] + (1, tiles.shape[-1]), tiles.dtype)
    after = jnp.concatenate([tiles[..., 1:, :], gap], axis=-2)
    before = jnp.concatenate([gap, tiles[..., :-1, :]], axis=-2)
    lane = lax.broadcasted_iota(jnp.int32, tiles.shape, tiles.ndim - 1)
    return jnp.where(lane < 64, after, before)


def under(tiles):
    gap = jnp.zeros(tiles.shape[:-2] + (1, tiles.shape[-1]), tiles.dtype)
    return jnp.concatenate([gap, tiles[..., :-1, :]], axis=-2)


def put(ref, index, tiles, second=beside):
    ref[index + (slice(None), slice(0, 128))] = tiles
    ref[index + (slice(None), slice(128, 256))] = second(tiles)


def flat(tiles):
    return tiles.reshape(-1, tiles.shape[-1])


def spaced(ref, a, rows, a_step, r, cols, r_step):
    lines = []
    for n in range(rows):
        if r_step == 1:
            lines.append(ref[a + a_step * n, r : r + cols])
        else:
            lines.append(jnp.stack([ref[a + a_step * n, r + r_step * m] for m in range(cols)]))
    return jnp.stack(lines)


def pair_dot(source, weights):
    total = None
    for slot in range(4):
        term = jnp.dot(flat(source(slot)), weights[slot], preferred_element_type=F32)
        total = term if total is None else total + term
    return leaky_relu(total)


def along_a(source, weights, a, pairs, r, count):
    total = pair_dot(lambda s: spaced(source, a - 1 + s, pairs, 2, r, count, 1), weights)
    return total.reshape(pairs, count, 16, 256)


def along_r(source, weights, a, count, r, pairs):
    total = pair_dot(lambda s: spaced(source, a, count, 1, r + s, pairs, 2), weights)
    return total.reshape(count, pairs, 16, 256)


def fill_p(xx, pp, weights, a, pairs, r, count):
    total = along_a(xx, weights, a, pairs, r + 1, count).astype(BF)
    for pair in range(pairs):
        for side in range(2):
            put(pp, (a + 2 * pair + side, slice(r + 1, r + 1 + count)), total[pair, :, :, 128 * side : 128 * side + 128])


def fill_q(xx, qq, weights, a, count, r, pairs):
    total = along_r(xx, weights, a, count, r, pairs).astype(BF)
    for pair in range(pairs):
        for side in range(2):
            put(qq, (slice(a, a + count), r + 2 * pair + side), total[:, pair, :, 128 * side : 128 * side + 128])


def fill_f(pp, qq, ff, part, wp, wq, a, a_pairs, r, r_pairs):
    count, span = 2 * a_pairs, 2 * r_pairs
    total = along_r(pp, wp, a, count, r, r_pairs)
    for pair in range(r_pairs):
        for side in range(2):
            part[0:count, 2 * pair + side] = total[:, pair, :, 128 * side : 128 * side + 128]
    total = along_a(qq, wq, a, a_pairs, r, span)
    for pair in range(a_pairs):
        for side in range(2):
            tiles = total[pair, :, :, 128 * side : 128 * side + 128] + part[2 * pair + side, 0:span]
            put(ff, (a + 2 * pair + side, slice(r + 1, r + 1 + span)), tiles.astype(BF), under)


def fill_g(ff, gg, w_oo, w_oe, w_eo, w_ee, a, rows, r, cols):
    def product(first_a, na, first_r, nr, weights):
        tiles = spaced(ff, first_a, na, 2, first_r + 1, nr, 2)
        total = jnp.dot(flat(tiles), weights[...], preferred_element_type=F32)
        return total.reshape(na, nr, 16, -1)

    odd = product(2 * a - 1, rows + 1, 2 * r - 1, cols + 1, w_oo)
    total = odd[:rows, :cols, :, 0:128] + odd[:rows, 1:, :, 128:256]
    total = total + (odd[1:, :cols, :, 256:384] + odd[1:, 1:, :, 384:512])
    mixed = product(2 * a - 1, rows + 1, 2 * r, cols, w_oe)
    total = total + (mixed[:rows, :, :, 0:128] + mixed[1:, :, :, 128:256])
    mixed = product(2 * a, rows, 2 * r - 1, cols + 1, w_eo)
    total = total + (mixed[:, :cols, :, 0:128] + mixed[:, 1:, :, 128:256])
    total = total + product(2 * a, rows, 2 * r, cols, w_ee)
    gg[a - 1 : a - 1 + rows, r + 1 : r + 1 + cols] = leaky_relu(total).astype(BF).astype(F32)


def tiles_kernel(x_hbm, tiles_ref, sector_ref, band_ref, corner_ref, x_ref, sems):
    rows = x_hbm.shape[0]
    copies = []
    for part in range(8):
        at = pl.ds(rows // 8 * part, rows // 8)
        copies.append(pltpu.make_async_copy(x_hbm.at[at], x_ref.at[at], sems.at[part]))
        copies[-1].start()
    for a in range(rows):
        if a % (rows // 8) == 0:
            copies[a // (rows // 8)].wait()
        tiles = x_ref[a].reshape(x_ref.shape[1], 16, 128)
        tiles_ref[a] = tiles
        band_ref[a] = tiles[:EDGE]
        if a < EDGE:
            sector_ref[a] = tiles
            corner_ref[a] = tiles[:EDGE]


def inner_kernel(
    tiles_ref, wp_hbm, wp2_hbm, wq_hbm, wq2_hbm, w1_hbm,
    wp, wp2, wq, wq2, w_oo, w_oe, w_eo, w_ee, xx, pp, qq, ff, gg,
    raw, raw1, part, sems,
):
    copies = [pltpu.make_async_copy(w, raw.at[n], sems.at[n]) for n, w in enumerate((wp_hbm, wq_hbm, wp2_hbm, wq2_hbm))]
    copies.append(pltpu.make_async_copy(w1_hbm, raw1, sems.at[4]))
    for copy in copies:
        copy.start()
    own = tiles_ref.shape[0]
    blank = jnp.zeros((1, 16, 256), BF)
    for a in range(own):
        put(xx, (a, slice(1, own + 1)), tiles_ref[a])
    for a in range(own + EDGE):
        xx[a, 0:1] = blank
        pp[a, 0:1] = blank
        ff[a, 0:1] = blank
    for a in range(9):
        gg[a, 0:1] = jnp.zeros((1, 16, 128), F32)
    xx[own + EDGE] = jnp.zeros(xx.shape[1:], BF)
    qq[own + EDGE] = jnp.zeros(qq.shape[1:], BF)

    zero = jnp.zeros((64, 64), BF)
    for n, out in enumerate((wp, wq, wp2, wq2)):
        copies[n].wait()
        for slot in range(4):
            for block, height in enumerate((0, 1, 2, -1)):
                for side in range(2):
                    tap = slot - side
                    parts = []
                    for upper in range(2):
                        k = height - upper + 1
                        inside = 0 <= tap <= 2 and 0 <= k <= 2
                        parts.append(raw[n, tap, k] if inside else zero)
                    out[slot, 64 * block : 64 * block + 64, 128 * side : 128 * side + 128] = (
                        jnp.concatenate(parts, axis=1)
                    )
    copies[4].wait()
    taps = (
        (w_oo, ((0, 0), (0, 2), (2, 0), (2, 2))), (w_oe, ((0, 1), (2, 1))), (w_eo, ((1, 0), (1, 2))), (w_ee, ((1, 1),)),
    )
    for out, pairs in taps:
        for n, (i, j) in enumerate(pairs):
            at = slice(128 * n, 128 * n + 128)
            out[0:64, at] = raw1[i, j, 1]
            out[64:128, at] = raw1[i, j, 2]
            out[128:192, at] = jnp.zeros((64, 128), BF)
            out[192:256, at] = raw1[i, j, 0]

    fill_p(xx, pp, wp, 1, 7, 0, 16)
    fill_q(xx, qq, wq, 0, 16, 0, 7)
    fill_f(pp, qq, ff, part, wp2, wq2, 1, 7, 0, 7)
    fill_g(ff, gg, w_oo, w_oe, w_eo, w_ee, 1, 6, 0, 7)


def outer_kernel(
    xx_in, pp_in, qq_in, ff_in, gg_in, sector_ref, band_ref, corner_ref,
    wp, wp2, wq, wq2, w_oo, w_oe, w_eo, w_ee, w2_ref,
    y_ref, xx, pp, qq, ff, gg, part, cells,
):
    own = band_ref.shape[0]
    for a in range(own):
        put(xx, (a, slice(own + 1, own + 1 + EDGE)), band_ref[a])
    for a in range(EDGE):
        put(xx, (own + a, slice(1, own + 1)), sector_ref[a])
        put(xx, (own + a, slice(own + 1, own + 1 + EDGE)), corner_ref[a])
    fill_p(xx, pp, wp, 1, 7, 16, 5)
    fill_p(xx, pp, wp, 15, 3, 0, 21)
    fill_q(xx, qq, wq, 0, 16, 14, 3)
    fill_q(xx, qq, wq, 16, 5, 0, 10)
    fill_f(pp, qq, ff, part, wp2, wq2, 1, 7, 14, 3)
    fill_f(pp, qq, ff, part, wp2, wq2, 15, 3, 0, 10)
    fill_g(ff, gg, w_oo, w_oe, w_eo, w_ee, 1, 6, 7, 3)
    fill_g(ff, gg, w_oo, w_oe, w_eo, w_ee, 7, 3, 0, 10)

    even = gg[:, :, pl.ds(0, 8, stride=2), :]
    odd = gg[:, :, pl.ds(1, 8, stride=2), :]
    cells[:, :, :, 0:128] = even
    cells[:, :, :, 128:256] = odd
    cells[:, :, :, 256:384] = under(odd)
    total = None
    for i in range(3):
        for j in range(3):
            rows = flat(spaced(cells, i, 4, 2, j, 5, 2)).astype(BF)
            term = jnp.dot(rows[:, 0:256], w2_ref[i, j, 1:3].reshape(256, 256), preferred_element_type=F32)
            term = term + jnp.dot(rows[:, 256:384], w2_ref[i, j, 0], preferred_element_type=F32)
            total = term if total is None else total + term
    y_ref[...] = leaky_relu(total).astype(BF)


def late_kernel(y_ref, coarse_hbm, coarse_out, spread_out, raw, sem):
    copy = pltpu.make_async_copy(coarse_hbm, raw, sem)
    copy.start()
    row = lax.broadcasted_iota(jnp.int32, (64, 512), 0)
    col = lax.broadcasted_iota(jnp.int32, (64, 512), 1)
    for h in range(8):
        spread_out[h] = jnp.where(col == row * 8 + h, 1.0, 0.0).astype(BF)
    band = lax.axis_index("blk")
    row = lax.broadcasted_iota(jnp.int32, (64, 256), 0)
    col = lax.broadcasted_iota(jnp.int32, (64, 256), 1)
    own = jnp.where(col == row + 64 * band, 1.0, 0.0).astype(BF)
    copy.wait()
    for i in range(3):
        for k in range(3):
            for j in range(3):
                coarse_out[i, k, 64 * j : 64 * j + 64] = raw[i, j, k]
            coarse_out[i, k, 192:256] = own if i == 1 and k == 1 else jnp.zeros((64, 256), BF)


def coarse_kernel_body(
    own_ref, near_ref, halo_ref, far_ref, far_halo_ref, last_ref, wc_ref, spread_ref, out_ref, slab, moved,
):
    band = lax.axis_index("blk")
    blocks = (
        (0, 2, own_ref[...]), (0, 0, halo_ref[...]), (1, 2, near_ref[...]), (1, 0, last_ref[0:80]),
        (2, 2, far_ref[...]), (2, 0, far_halo_ref[...]), (3, 2, last_ref[80:240]), (3, 0, last_ref[240:320]),
    )
    for place, first, block in blocks:
        other = jnp.bitwise_xor(band, place)
        block = block.astype(F32).reshape(-1, 5, 8, 256)
        at = slice(first, first + block.shape[0])
        slab[at, pl.ds(4 * other + 1, 4)] = block[:, 1:5]

        @pl.when(other == 0)
        def _():
            slab[at, 0:1] = block[:, 0:1]

    for a in range(4):
        rows = [slab[a + i, 0:16].astype(BF).reshape(128, 256) for i in range(3)]
        tall = None
        for k in range(3):
            total = None
            for i in range(3):
                term = lax.dot_general(rows[i], wc_ref[i, k], (((1,), (1,)), ((), ())), preferred_element_type=F32)
                total = term if total is None else total + term
            total = total.reshape(16, 8, 256)
            gap = jnp.zeros((16, 1, 256), F32)
            if k == 0:
                total = jnp.concatenate([gap, total[:, :-1]], axis=1)
            elif k == 2:
                total = jnp.concatenate([total[:, 1:], gap], axis=1)
            else:
                kept = total[:, :, 192:256]
            tall = total if tall is None else tall + total
        gap = jnp.zeros((1, 8, 64), F32)
        total = (
            jnp.concatenate([gap, tall[:-1, :, 0:64]], axis=0)
            + tall[:, :, 64:128]
            + jnp.concatenate([tall[1:, :, 128:192], gap], axis=0)
        )
        moved[128 * a : 128 * a + 128, 0:64] = (kept + leaky_relu(total)).reshape(128, 64)
    total = None
    for h in range(8):
        rows = moved[pl.ds(h, 64, stride=8), :].astype(BF)
        term = jnp.dot(rows[:, 0:64], spread_ref[h], preferred_element_type=F32)
        total = term if total is None else total + term
    out_ref[...] = total.astype(BF).reshape(4, 16, 512)


def moved_by(x, sectors, band_of):
    count, bands = lax.axis_size("sector"), lax.axis_size("blk")
    pairs = []
    for s in range(count):
        for b in range(bands):
            if 0 <= band_of(b) < bands:
                pairs.append((s * bands + b, (s + sectors) % count * bands + band_of(b)))
    return lax.ppermute(x, ("sector", "blk"), pairs)


def shaped(*dims, dtype=BF):
    return jax.ShapeDtypeStruct(dims, dtype)


def run(kernel, outs, scratch, flops, name, *args, limit=24, hbm=(), aliases=None):
    return pl.pallas_call(
        kernel,
        out_shape=outs,
        in_specs=[pl.BlockSpec(memory_space=pl.ANY) if n in hbm else VMEM for n in range(len(args))],
        out_specs=jax.tree.map(lambda _: VMEM, outs),
        scratch_shapes=scratch,
        input_output_aliases=aliases or {},
        compiler_params=pltpu.CompilerParams(vmem_limit_bytes=limit << 20),
        cost_estimate=pl.CostEstimate(flops=flops, bytes_accessed=1 << 20, transcendentals=0),
        name=name,
    )(*args)


def per_device(features, residual_first, residual_second, shortcut_first, shortcut_second,
               first_reduce_weight, second_reduce_weight, coarse_kernel):
    tiles, sector_edge, band_edge, corner = run(
        tiles_kernel,
        (shaped(16, 16, 16, 128), shaped(EDGE, 16, 16, 128), shaped(16, EDGE, 16, 128), shaped(EDGE, EDGE, 16, 128)),
        (pltpu.VMEM((16, 16, 2048), BF), pltpu.SemaphoreType.DMA((8,))),
        1 << 30, "tiles", features, limit=8, hbm=(0,),
    )
    sector_edge = moved_by(sector_edge, -1, lambda b: b)
    band_edge = moved_by(band_edge, 0, lambda b: b - 1)
    corner = moved_by(corner, -1, lambda b: b - 1)
    held = (
        shaped(22, 22, 16, 256), shaped(21, 22, 16, 256), shaped(22, 20, 16, 256), shaped(21, 21, 16, 256),
        shaped(9, 11, 16, 128, dtype=F32),
    )
    made = run(
        inner_kernel,
        (shaped(4, 256, 256),) * 4 + (shaped(256, 512), shaped(256, 256), shaped(256, 256), shaped(256, 128)) + held,
        (
            pltpu.VMEM((4, 3, 3, 64, 64), BF),
            pltpu.VMEM((3, 3, 3, 64, 128), BF),
            pltpu.VMEM((14, 14, 16, 128), F32),
            pltpu.SemaphoreType.DMA((5,)),
        ),
        6 << 30, "inner", tiles,
        residual_first, residual_second, shortcut_first, shortcut_second, first_reduce_weight,
        hbm=(1, 2, 3, 4, 5),
    )
    weights, levels = made[:8], made[8:]
    y, *_ = run(
        outer_kernel,
        (shaped(160, 256),) + held,
        (pltpu.VMEM((14, 20, 16, 128), F32), pltpu.VMEM((9, 11, 8, 384), F32)),
        6 << 30, "outer", *levels, sector_edge, band_edge, corner, *weights, second_reduce_weight,
        aliases={n: n + 1 for n in range(5)},
    )
    halo = moved_by(y[80:160], 1, lambda b: b)
    far = moved_by(y, 0, lambda b: b ^ 2)
    near = moved_by(y, 0, lambda b: b ^ 1)
    far_halo = moved_by(halo, 0, lambda b: b ^ 2)
    last = moved_by(jnp.concatenate([halo, far, far_halo], axis=0), 0, lambda b: b ^ 1)
    wc, spread = run(
        late_kernel,
        (shaped(3, 3, 256, 256), shaped(8, 64, 512)),
        (pltpu.VMEM((3, 3, 3, 64, 256), BF), pltpu.SemaphoreType.DMA),
        1 << 30, "late", y, jnp.swapaxes(coarse_kernel, 3, 4), limit=8, hbm=(1,),
    )
    return run(
        coarse_kernel_body,
        shaped(4, 16, 512),
        (pltpu.VMEM((6, 18, 8, 256), F32), pltpu.VMEM((512, 128), F32)),
        2 << 30, "coarse", y, near, halo, far, far_halo, last, wc, spread, limit=16,
    )


def solution(mesh):
    in_specs = (P("sector", "blk", None),) + (P(),) * 6 + (P(None, None, None, None, "blk"),)
    return jax.shard_map(
        per_device, mesh=mesh, in_specs=in_specs, out_specs=P("sector", None, "blk"), check_vma=False
    )
```

```python
import jax
import jax.numpy as jnp
from jax import lax
from jax.experimental import pallas as pl
from jax.experimental.pallas import tpu as pltpu
from jax.sharding import PartitionSpec as P

BF = jnp.bfloat16
F32 = jnp.float32
EDGE = 5
VMEM = pl.BlockSpec(memory_space=pltpu.VMEM)


def leaky_relu(values):
    return jnp.maximum(values, 0.01 * values)


def beside(tiles):
    gap = jnp.zeros(tiles.shape[:-2] + (1, tiles.shape[-1]), tiles.dtype)
    after = jnp.concatenate([tiles[..., 1:, :], gap], axis=-2)
    before = jnp.concatenate([gap, tiles[..., :-1, :]], axis=-2)
    lane = lax.broadcasted_iota(jnp.int32, tiles.shape, tiles.ndim - 1)
    return jnp.where(lane < 64, after, before)


def under(tiles):
    gap = jnp.zeros(tiles.shape[:-2] + (1, tiles.shape[-1]), tiles.dtype)
    return jnp.concatenate([gap, tiles[..., :-1, :]], axis=-2)


def put(ref, index, tiles, second=beside):
    ref[index + (slice(None), slice(0, 128))] = tiles
    ref[index + (slice(None), slice(128, 256))] = second(tiles)


def flat(tiles):
    return tiles.reshape(-1, tiles.shape[-1])


def spaced(ref, a, rows, a_step, r, cols, r_step):
    lines = []
    for n in range(rows):
        if r_step == 1:
            lines.append(ref[a + a_step * n, r : r + cols])
        else:
            lines.append(jnp.stack([ref[a + a_step * n, r + r_step * m] for m in range(cols)]))
    return jnp.stack(lines)


def pair_dot(source, weights):
    total = None
    for slot in range(4):
        term = jnp.dot(flat(source(slot)), weights[slot], preferred_element_type=F32)
        total = term if total is None else total + term
    return leaky_relu(total)


def along_a(source, weights, a, pairs, r, count):
    total = pair_dot(lambda s: spaced(source, a - 1 + s, pairs, 2, r, count, 1), weights)
    return total.reshape(pairs, count, 16, 256)


def along_r(source, weights, a, count, r, pairs):
    total = pair_dot(lambda s: spaced(source, a, count, 1, r + s, pairs, 2), weights)
    return total.reshape(count, pairs, 16, 256)


def fill_p(xx, pp, weights, a, pairs, r, count):
    total = along_a(xx, weights, a, pairs, r + 1, count).astype(BF)
    for pair in range(pairs):
        for side in range(2):
            put(pp, (a + 2 * pair + side, slice(r + 1, r + 1 + count)), total[pair, :, :, 128 * side : 128 * side + 128])


def fill_q(xx, qq, weights, a, count, r, pairs):
    total = along_r(xx, weights, a, count, r, pairs).astype(BF)
    for pair in range(pairs):
        for side in range(2):
            put(qq, (slice(a, a + count), r + 2 * pair + side), total[:, pair, :, 128 * side : 128 * side + 128])


def fill_f(pp, qq, ff, part, wp, wq, a, a_pairs, r, r_pairs):
    count, span = 2 * a_pairs, 2 * r_pairs
    total = along_r(pp, wp, a, count, r, r_pairs)
    for pair in range(r_pairs):
        for side in range(2):
            part[0:count, 2 * pair + side] = total[:, pair, :, 128 * side : 128 * side + 128]
    total = along_a(qq, wq, a, a_pairs, r, span)
    for pair in range(a_pairs):
        for side in range(2):
            tiles = total[pair, :, :, 128 * side : 128 * side + 128] + part[2 * pair + side, 0:span]
            put(ff, (a + 2 * pair + side, slice(r + 1, r + 1 + span)), tiles.astype(BF), under)


def fill_g(ff, gg, w_oo, w_oe, w_eo, w_ee, a, rows, r, cols):
    def product(first_a, na, first_r, nr, weights):
        tiles = spaced(ff, first_a, na, 2, first_r + 1, nr, 2)
        total = jnp.dot(flat(tiles), weights[...], preferred_element_type=F32)
        return total.reshape(na, nr, 16, -1)

    odd = product(2 * a - 1, rows + 1, 2 * r - 1, cols + 1, w_oo)
    total = odd[:rows, :cols, :, 0:128] + odd[:rows, 1:, :, 128:256]
    total = total + (odd[1:, :cols, :, 256:384] + odd[1:, 1:, :, 384:512])
    mixed = product(2 * a - 1, rows + 1, 2 * r, cols, w_oe)
    total = total + (mixed[:rows, :, :, 0:128] + mixed[1:, :, :, 128:256])
    mixed = product(2 * a, rows, 2 * r - 1, cols + 1, w_eo)
    total = total + (mixed[:, :cols, :, 0:128] + mixed[:, 1:, :, 128:256])
    total = total + product(2 * a, rows, 2 * r, cols, w_ee)
    gg[a - 1 : a - 1 + rows, r + 1 : r + 1 + cols] = leaky_relu(total).astype(BF).astype(F32)


def band_edge_kernel(x_ref, band_ref):
    for a in range(x_ref.shape[0]):
        band_ref[a] = x_ref[a, 0:8].reshape(8, 16, 128)[:EDGE]


def sector_edge_kernel(x_ref, band_ref, sector_ref, corner_ref):
    for a in range(EDGE):
        sector_ref[a] = x_ref[a].reshape(x_ref.shape[1], 16, 128)
        corner_ref[a] = band_ref[a]


def inner_kernel(
    x_ref, wp_raw, wp2_raw, wq_raw, wq2_raw, w1_raw,
    wp, wp2, wq, wq2, w_oo, w_oe, w_eo, w_ee, xx, pp, qq, ff, gg,
    part,
):
    own = x_ref.shape[0]
    blank = jnp.zeros((1, 16, 256), BF)
    for a in range(own + EDGE):
        xx[a, 0:1] = blank
        pp[a, 0:1] = blank
        ff[a, 0:1] = blank
    for a in range(9):
        gg[a, 0:1] = jnp.zeros((1, 16, 128), F32)
    xx[own + EDGE] = jnp.zeros(xx.shape[1:], BF)
    qq[own + EDGE] = jnp.zeros(qq.shape[1:], BF)
    for a in range(own):
        put(xx, (a, slice(1, own + 1)), x_ref[a].reshape(own, 16, 128))

    zero = jnp.zeros((64, 64), BF)
    for raw, out in ((wp_raw, wp), (wq_raw, wq), (wp2_raw, wp2), (wq2_raw, wq2)):
        for slot in range(4):
            for block, height in enumerate((0, 1, 2, -1)):
                for side in range(2):
                    tap = slot - side
                    parts = []
                    for upper in range(2):
                        k = height - upper + 1
                        inside = 0 <= tap <= 2 and 0 <= k <= 2
                        parts.append(raw[tap, k] if inside else zero)
                    out[slot, 64 * block : 64 * block + 64, 128 * side : 128 * side + 128] = (
                        jnp.concatenate(parts, axis=1)
                    )
    taps = (
        (w_oo, ((0, 0), (0, 2), (2, 0), (2, 2))), (w_oe, ((0, 1), (2, 1))), (w_eo, ((1, 0), (1, 2))), (w_ee, ((1, 1),)),
    )
    for out, pairs in taps:
        for n, (i, j) in enumerate(pairs):
            at = slice(128 * n, 128 * n + 128)
            out[0:64, at] = w1_raw[i, j, 1]
            out[64:128, at] = w1_raw[i, j, 2]
            out[128:192, at] = jnp.zeros((64, 128), BF)
            out[192:256, at] = w1_raw[i, j, 0]

    fill_p(xx, pp, wp, 1, 7, 0, 16)
    fill_q(xx, qq, wq, 0, 16, 0, 7)
    fill_f(pp, qq, ff, part, wp2, wq2, 1, 7, 0, 7)
    fill_g(ff, gg, w_oo, w_oe, w_eo, w_ee, 1, 6, 0, 7)


def band_kernel(
    xx_in, pp_in, qq_in, ff_in, gg_in, band_ref,
    wp, wp2, wq, wq2, w_oo, w_oe, w_eo, w_ee,
    xx, pp, qq, ff, gg, part,
):
    own = band_ref.shape[0]
    for a in range(own):
        put(xx, (a, slice(own + 1, own + 1 + EDGE)), band_ref[a])
    fill_p(xx, pp, wp, 1, 7, 16, 5)
    fill_q(xx, qq, wq, 0, 16, 14, 3)
    fill_f(pp, qq, ff, part, wp2, wq2, 1, 7, 14, 3)
    fill_g(ff, gg, w_oo, w_oe, w_eo, w_ee, 1, 6, 7, 3)


def outer_kernel(
    xx_in, pp_in, qq_in, ff_in, gg_in, sector_ref, corner_ref,
    wp, wp2, wq, wq2, w_oo, w_oe, w_eo, w_ee, w2_ref,
    y_ref, xx, pp, qq, ff, gg, part, cells,
):
    own = sector_ref.shape[1]
    for a in range(EDGE):
        put(xx, (own + a, slice(1, own + 1)), sector_ref[a])
        put(xx, (own + a, slice(own + 1, own + 1 + EDGE)), corner_ref[a])
    fill_p(xx, pp, wp, 15, 3, 0, 21)
    fill_q(xx, qq, wq, 16, 5, 0, 10)
    fill_f(pp, qq, ff, part, wp2, wq2, 15, 3, 0, 10)
    fill_g(ff, gg, w_oo, w_oe, w_eo, w_ee, 7, 3, 0, 10)

    even = gg[:, :, pl.ds(0, 8, stride=2), :]
    odd = gg[:, :, pl.ds(1, 8, stride=2), :]
    cells[:, :, :, 0:128] = even
    cells[:, :, :, 128:256] = odd
    cells[:, :, :, 256:384] = under(odd)
    total = None
    for i in range(3):
        for j in range(3):
            rows = flat(spaced(cells, i, 4, 2, j, 5, 2)).astype(BF)
            term = jnp.dot(rows[:, 0:256], w2_ref[i, j, 1:3].reshape(256, 256), preferred_element_type=F32)
            term = term + jnp.dot(rows[:, 256:384], w2_ref[i, j, 0], preferred_element_type=F32)
            total = term if total is None else total + term
    y_ref[...] = leaky_relu(total).astype(BF)


def late_kernel(y_ref, raw, coarse_out, spread_out):
    row = lax.broadcasted_iota(jnp.int32, (64, 512), 0)
    col = lax.broadcasted_iota(jnp.int32, (64, 512), 1)
    for h in range(8):
        spread_out[h] = jnp.where(col == row * 8 + h, 1.0, 0.0).astype(BF)
    band = lax.axis_index("blk")
    row = lax.broadcasted_iota(jnp.int32, (64, 256), 0)
    col = lax.broadcasted_iota(jnp.int32, (64, 256), 1)
    own = jnp.where(col == row + 64 * band, 1.0, 0.0).astype(BF)
    for i in range(3):
        for k in range(3):
            last = own if i == 1 and k == 1 else jnp.zeros((64, 256), BF)
            coarse_out[i, k] = jnp.concatenate([raw[i, 0, k], raw[i, 1, k], raw[i, 2, k], last], axis=0).T


def coarse_kernel_body(
    own_ref, near_ref, halo_ref, far_ref, far_halo_ref, last_ref, wc_ref, spread_ref, out_ref, slab, moved,
):
    band = lax.axis_index("blk")
    blocks = (
        (0, 2, own_ref[...]), (0, 0, halo_ref[...]), (1, 2, near_ref[...]), (1, 0, last_ref[0:80]),
        (2, 2, far_ref[...]), (2, 0, far_halo_ref[...]), (3, 2, last_ref[80:240]), (3, 0, last_ref[240:320]),
    )
    for place, first, block in blocks:
        other = jnp.bitwise_xor(band, place)
        block = block.astype(F32).reshape(-1, 5, 8, 256)
        at = slice(first, first + block.shape[0])
        slab[at, pl.ds(4 * other + 1, 4)] = block[:, 1:5]

        @pl.when(other == 0)
        def _():
            slab[at, 0:1] = block[:, 0:1]

    for a in range(4):
        rows = [slab[a + i, 0:16].astype(BF).reshape(128, 256) for i in range(3)]
        tall = None
        for k in range(3):
            total = None
            for i in range(3):
                term = jnp.dot(rows[i], wc_ref[i, k], preferred_element_type=F32)
                total = term if total is None else total + term
            total = total.reshape(16, 8, 256)
            gap = jnp.zeros((16, 1, 256), F32)
            if k == 0:
                total = jnp.concatenate([gap, total[:, :-1]], axis=1)
            elif k == 2:
                total = jnp.concatenate([total[:, 1:], gap], axis=1)
            else:
                kept = total[:, :, 192:256]
            tall = total if tall is None else tall + total
        gap = jnp.zeros((1, 8, 64), F32)
        total = (
            jnp.concatenate([gap, tall[:-1, :, 0:64]], axis=0)
            + tall[:, :, 64:128]
            + jnp.concatenate([tall[1:, :, 128:192], gap], axis=0)
        )
        moved[128 * a : 128 * a + 128, 0:64] = (kept + leaky_relu(total)).reshape(128, 64)
    total = None
    for h in range(8):
        rows = moved[pl.ds(h, 64, stride=8), :].astype(BF)
        term = jnp.dot(rows[:, 0:64], spread_ref[h], preferred_element_type=F32)
        total = term if total is None else total + term
    out_ref[...] = total.astype(BF).reshape(4, 16, 512)


def moved_by(x, sectors, band_of):
    count, bands = lax.axis_size("sector"), lax.axis_size("blk")
    pairs = []
    for s in range(count):
        for b in range(bands):
            if 0 <= band_of(b) < bands:
                pairs.append((s * bands + b, (s + sectors) % count * bands + band_of(b)))
    return lax.ppermute(x, ("sector", "blk"), pairs)


def shaped(*dims, dtype=BF):
    return jax.ShapeDtypeStruct(dims, dtype)


def run(kernel, outs, scratch, flops, name, *args, limit=24, hbm=(), aliases=None):
    return pl.pallas_call(
        kernel,
        out_shape=outs,
        in_specs=[pl.BlockSpec(memory_space=pltpu.HBM) if n in hbm else VMEM for n in range(len(args))],
        out_specs=jax.tree.map(lambda _: VMEM, outs),
        scratch_shapes=scratch,
        input_output_aliases=aliases or {},
        compiler_params=pltpu.CompilerParams(vmem_limit_bytes=limit << 20),
        cost_estimate=pl.CostEstimate(flops=flops, bytes_accessed=1 << 20, transcendentals=0),
        name=name,
    )(*args)


def per_device(features, residual_first, residual_second, shortcut_first, shortcut_second,
               first_reduce_weight, second_reduce_weight, coarse_kernel):
    own_band = run(band_edge_kernel, shaped(16, EDGE, 16, 128), (), 2 << 30, "band_edge", features)
    band_edge = moved_by(own_band, 0, lambda b: b - 1)
    sector_edge, corner = run(
        sector_edge_kernel, (shaped(EDGE, 16, 16, 128), shaped(EDGE, EDGE, 16, 128)), (), 4 << 30,
        "sector_edge", features, own_band,
    )
    sector_edge = moved_by(sector_edge, -1, lambda b: b)
    corner = moved_by(corner, -1, lambda b: b - 1)
    held = (
        shaped(22, 22, 16, 256), shaped(21, 22, 16, 256), shaped(22, 20, 16, 256), shaped(21, 21, 16, 256),
        shaped(9, 11, 16, 128, dtype=F32),
    )
    made = run(
        inner_kernel,
        (shaped(4, 256, 256),) * 4 + (shaped(256, 512), shaped(256, 256), shaped(256, 256), shaped(256, 128)) + held,
        (
            pltpu.VMEM((14, 14, 16, 128), F32),
        ),
        6 << 30, "inner", features,
        residual_first, residual_second, shortcut_first, shortcut_second, first_reduce_weight,
    )
    weights, levels = made[:8], made[8:]
    levels = run(
        band_kernel, held, (pltpu.VMEM((14, 6, 16, 128), F32),),
        3 << 30, "band", *levels, band_edge, *weights,
        aliases={n: n for n in range(5)},
    )
    *levels, sector_edge, corner = lax.optimization_barrier((*levels, sector_edge, corner))
    y, *_ = run(
        outer_kernel,
        (shaped(160, 256),) + held,
        (pltpu.VMEM((6, 20, 16, 128), F32), pltpu.VMEM((9, 11, 8, 384), F32)),
        4 << 30, "outer", *levels, sector_edge, corner, *weights, second_reduce_weight,
        aliases={n: n + 1 for n in range(5)},
    )
    far = moved_by(y, 0, lambda b: b ^ 2)
    halo = moved_by(y[80:160], 1, lambda b: b)
    far_halo = moved_by(y[80:160], 1, lambda b: b ^ 2)
    near = moved_by(y, 0, lambda b: b ^ 1)
    wc, spread = run(
        late_kernel,
        (shaped(3, 3, 256, 256), shaped(8, 64, 512)),
        (), 4 << 30, "late", y, jnp.swapaxes(coarse_kernel, 3, 4), limit=8,
    )
    far, near, halo, far_halo, wc, spread = lax.optimization_barrier((far, near, halo, far_halo, wc, spread))
    last = moved_by(jnp.concatenate([halo, far, far_halo], axis=0), 0, lambda b: b ^ 1)
    return run(
        coarse_kernel_body,
        shaped(4, 16, 512),
        (pltpu.VMEM((6, 18, 8, 256), F32), pltpu.VMEM((512, 128), F32)),
        2 << 30, "coarse", y, near, halo, far, far_halo, last, wc, spread, limit=16,
    )


def solution(mesh):
    in_specs = (P("sector", "blk", None),) + (P(),) * 6 + (P(None, None, None, None, "blk"),)
    return jax.shard_map(
        per_device, mesh=mesh, in_specs=in_specs, out_specs=P("sector", None, "blk"), check_vma=False
    )
```

```python
import jax
import jax.numpy as jnp
from jax import lax
from jax.experimental import pallas as pl
from jax.experimental.pallas import tpu as pltpu
from jax.sharding import PartitionSpec as P

BF = jnp.bfloat16
F32 = jnp.float32
ROWS = 5
EDGE = 5
VMEM = pl.BlockSpec(memory_space=pltpu.VMEM)


def leaky_relu(values):
    return jnp.maximum(values, 0.01 * values)


def beside(tiles):
    gap = jnp.zeros(tiles.shape[:-2] + (1, tiles.shape[-1]), tiles.dtype)
    after = jnp.concatenate([tiles[..., 1:, :], gap], axis=-2)
    before = jnp.concatenate([gap, tiles[..., :-1, :]], axis=-2)
    lane = lax.broadcasted_iota(jnp.int32, tiles.shape, tiles.ndim - 1)
    return jnp.where(lane < 64, after, before)


def under(tiles):
    gap = jnp.zeros(tiles.shape[:-2] + (1, tiles.shape[-1]), tiles.dtype)
    return jnp.concatenate([gap, tiles[..., :-1, :]], axis=-2)


def put(ref, index, tiles, second=beside):
    ref[index + (slice(None), slice(0, 128))] = tiles
    ref[index + (slice(None), slice(128, 256))] = second(tiles)


def flat(tiles):
    return tiles.reshape(-1, tiles.shape[-1])


def spaced(ref, a, rows, a_step, r, cols, r_step):
    lines = []
    for n in range(rows):
        if r_step == 1:
            lines.append(ref[a + a_step * n, r : r + cols])
        else:
            lines.append(jnp.stack([ref[a + a_step * n, r + r_step * m] for m in range(cols)]))
    return jnp.stack(lines)


def pair_dot(source, weights):
    total = None
    for slot in range(4):
        term = jnp.dot(flat(source(slot)), weights[slot], preferred_element_type=F32)
        total = term if total is None else total + term
    return leaky_relu(total)


def along_a(source, weights, a, pairs, r, count):
    total = pair_dot(lambda s: spaced(source, a - 1 + s, pairs, 2, r, count, 1), weights)
    return total.reshape(pairs, count, 16, 256)


def along_r(source, weights, a, count, r, pairs):
    total = pair_dot(lambda s: spaced(source, a, count, 1, r + s, pairs, 2), weights)
    return total.reshape(count, pairs, 16, 256)


def fill_p(xx, pp, weights, a, pairs, r, count):
    for pair in range(pairs):
        for first in range(0, count, 8):
            width = min(8, count - first)
            total = along_a(xx, weights, a + 2 * pair, 1, r + 1 + first, width).astype(BF)[0]
            at = slice(r + 1 + first, r + 1 + first + width)
            for side in range(2):
                put(pp, (a + 2 * pair + side, at), total[:, :, 128 * side : 128 * side + 128])


def fill_q(xx, qq, weights, a, count, r, pairs, step):
    for first in range(a, a + count, step):
        rows = min(step, a + count - first)
        total = along_r(xx, weights, first, rows, r, pairs).astype(BF)
        for pair in range(pairs):
            for side in range(2):
                put(qq, (slice(first, first + rows), r + 2 * pair + side), total[:, pair, :, 128 * side : 128 * side + 128])


def fill_f(pp, qq, ff, part, wp, wq, a, a_pairs, r, r_pairs):
    count, span = 2 * a_pairs, 2 * r_pairs
    total = along_r(pp, wp, a, count, r, r_pairs)
    for pair in range(r_pairs):
        for side in range(2):
            part[0:count, 2 * pair + side] = total[:, pair, :, 128 * side : 128 * side + 128]
    total = along_a(qq, wq, a, a_pairs, r, span)
    for pair in range(a_pairs):
        for side in range(2):
            tiles = total[pair, :, :, 128 * side : 128 * side + 128] + part[2 * pair + side, 0:span]
            put(ff, (a + 2 * pair + side, slice(r + 1, r + 1 + span)), tiles.astype(BF), under)


def fill_g(ff, gg, w_oo, w_oe, w_eo, w_ee, a, rows, r, cols):
    def product(first_a, na, first_r, nr, weights):
        tiles = spaced(ff, first_a, na, 2, first_r + 1, nr, 2)
        total = jnp.dot(flat(tiles), weights[...], preferred_element_type=F32)
        return total.reshape(na, nr, 16, -1)

    odd = product(2 * a - 1, rows + 1, 2 * r - 1, cols + 1, w_oo)
    total = odd[:rows, :cols, :, 0:128] + odd[:rows, 1:, :, 128:256]
    total = total + (odd[1:, :cols, :, 256:384] + odd[1:, 1:, :, 384:512])
    mixed = product(2 * a - 1, rows + 1, 2 * r, cols, w_oe)
    total = total + (mixed[:rows, :, :, 0:128] + mixed[1:, :, :, 128:256])
    mixed = product(2 * a, rows, 2 * r - 1, cols + 1, w_eo)
    total = total + (mixed[:, :cols, :, 0:128] + mixed[:, 1:, :, 128:256])
    total = total + product(2 * a, rows, 2 * r, cols, w_ee)
    gg[a - 1 : a - 1 + rows, r + 1 : r + 1 + cols] = leaky_relu(total).astype(BF).astype(F32)


def band_edge_kernel(x_ref, band_ref):
    for a in range(x_ref.shape[0]):
        band_ref[a] = x_ref[a, 0:8].reshape(8, 16, 128)[:EDGE]


def sector_edge_kernel(x_ref, band_ref, sector_ref, corner_ref):
    for a in range(ROWS):
        sector_ref[a] = x_ref[a].reshape(x_ref.shape[1], 16, 128)
        corner_ref[a] = band_ref[a]


def inner_kernel(
    x_ref, wp_raw, wp2_raw, wq_raw, wq2_raw, w1_raw,
    wp, wp2, wq, wq2, w_oo, w_oe, w_eo, w_ee, xx, pp, qq, ff, gg,
    part,
):
    own = x_ref.shape[0]
    blank = jnp.zeros((1, 16, 256), BF)
    for a in range(own + ROWS):
        xx[a, 0:1] = blank
        pp[a, 0:1] = blank
        ff[a, 0:1] = blank
    for a in range(9):
        gg[a, 0:1] = jnp.zeros((1, 16, 128), F32)
    xx[own + ROWS] = jnp.zeros(xx.shape[1:], BF)
    qq[own + ROWS] = jnp.zeros(qq.shape[1:], BF)
    for a in range(own):
        put(xx, (a, slice(1, own + 1)), x_ref[a].reshape(own, 16, 128))

    zero = jnp.zeros((64, 64), BF)
    for raw, out in ((wp_raw, wp), (wq_raw, wq), (wp2_raw, wp2), (wq2_raw, wq2)):
        for slot in range(4):
            for block, height in enumerate((0, 1, 2, -1)):
                for side in range(2):
                    tap = slot - side
                    parts = []
                    for upper in range(2):
                        k = height - upper + 1
                        inside = 0 <= tap <= 2 and 0 <= k <= 2
                        parts.append(raw[tap, k] if inside else zero)
                    out[slot, 64 * block : 64 * block + 64, 128 * side : 128 * side + 128] = (
                        jnp.concatenate(parts, axis=1)
                    )
    taps = (
        (w_oo, ((0, 0), (0, 2), (2, 0), (2, 2))), (w_oe, ((0, 1), (2, 1))), (w_eo, ((1, 0), (1, 2))), (w_ee, ((1, 1),)),
    )
    for out, pairs in taps:
        for n, (i, j) in enumerate(pairs):
            at = slice(128 * n, 128 * n + 128)
            out[0:64, at] = w1_raw[i, j, 1]
            out[64:128, at] = w1_raw[i, j, 2]
            out[128:192, at] = jnp.zeros((64, 128), BF)
            out[192:256, at] = w1_raw[i, j, 0]

    fill_p(xx, pp, wp, 1, 7, 0, 16)
    fill_q(xx, qq, wq, 0, 16, 0, 7, 2)
    for pair in range(7):
        fill_f(pp, qq, ff, part, wp2, wq2, 1 + 2 * pair, 1, 0, 7)
    fill_g(ff, gg, w_oo, w_oe, w_eo, w_ee, 1, 6, 0, 7)


def band_kernel(
    xx_in, pp_in, qq_in, ff_in, gg_in, band_ref,
    wp, wp2, wq, wq2, w_oo, w_oe, w_eo, w_ee,
    xx, pp, qq, ff, gg, part,
):
    own = band_ref.shape[0]
    for a in range(own):
        put(xx, (a, slice(own + 1, own + 1 + EDGE)), band_ref[a])
    total = along_a(xx, wp, 1, 7, 17, EDGE).astype(BF)
    for pair in range(7):
        for side in range(2):
            put(pp, (1 + 2 * pair + side, slice(17, 17 + EDGE)), total[pair, :, :, 128 * side : 128 * side + 128])
    fill_q(xx, qq, wq, 0, 16, 14, 3, 8)
    fill_f(pp, qq, ff, part, wp2, wq2, 1, 7, 14, 3)
    fill_g(ff, gg, w_oo, w_oe, w_eo, w_ee, 1, 6, 7, 3)


def outer_kernel(
    xx_in, pp_in, qq_in, ff_in, gg_in, sector_ref, corner_ref,
    wp, wp2, wq, wq2, w_oo, w_oe, w_eo, w_ee, w2_ref,
    y_ref, xx, pp, qq, ff, gg, part, cells,
):
    own = sector_ref.shape[1]
    for a in range(ROWS):
        put(xx, (own + a, slice(1, own + 1)), sector_ref[a])
        put(xx, (own + a, slice(own + 1, own + 1 + EDGE)), corner_ref[a])
    fill_p(xx, pp, wp, 15, 3, 0, 21)
    fill_q(xx, qq, wq, 16, 5, 0, 10, 1)
    for pair in range(3):
        fill_f(pp, qq, ff, part, wp2, wq2, 15 + 2 * pair, 1, 0, 10)
    fill_g(ff, gg, w_oo, w_oe, w_eo, w_ee, 7, 3, 0, 10)
    even = gg[:, :, pl.ds(0, 8, stride=2), :]
    odd = gg[:, :, pl.ds(1, 8, stride=2), :]
    cells[:, :, :, 0:128] = even
    cells[:, :, :, 128:256] = odd
    cells[:, :, :, 256:384] = under(odd)
    total = None
    for i in range(3):
        for j in range(3):
            rows = flat(spaced(cells, i, 4, 2, j, 5, 2)).astype(BF)
            term = jnp.dot(rows[:, 0:256], w2_ref[i, j, 1:3].reshape(256, 256), preferred_element_type=F32)
            term = term + jnp.dot(rows[:, 256:384], w2_ref[i, j, 0], preferred_element_type=F32)
            total = term if total is None else total + term
    y_ref[...] = leaky_relu(total).astype(BF)


def late_kernel(y_ref, raw, coarse_out, spread_out):
    row = lax.broadcasted_iota(jnp.int32, (64, 512), 0)
    col = lax.broadcasted_iota(jnp.int32, (64, 512), 1)
    for h in range(8):
        spread_out[h] = jnp.where(col == row * 8 + h, 1.0, 0.0).astype(BF)
    band = lax.axis_index("blk")
    row = lax.broadcasted_iota(jnp.int32, (64, 256), 0)
    col = lax.broadcasted_iota(jnp.int32, (64, 256), 1)
    own = jnp.where(col == row + 64 * band, 1.0, 0.0).astype(BF)
    for i in range(3):
        for k in range(3):
            last = own if i == 1 and k == 1 else jnp.zeros((64, 256), BF)
            coarse_out[i, k] = jnp.concatenate([raw[i, 0, k], raw[i, 1, k], raw[i, 2, k], last], axis=0).T


def lay(slab, first, other, block):
    block = block.astype(F32).reshape(-1, 5, 8, 256)
    at = slice(first, first + block.shape[0])
    slab[at, pl.ds(4 * other + 1, 4)] = block[:, 1:5]

    @pl.when(other == 0)
    def _():
        slab[at, 0:1] = block[:, 0:1]


def coarse_rows(slab, wc_ref, spread_ref, moved, first, count):
    cast = [slab[a, 0:16].astype(BF).reshape(128, 256) for a in range(first, first + count + 2)]
    for n in range(count):
        tall = None
        for k in range(3):
            total = None
            for i in range(3):
                term = jnp.dot(cast[n + i], wc_ref[i, k], preferred_element_type=F32)
                total = term if total is None else total + term
            total = total.reshape(16, 8, 256)
            gap = jnp.zeros((16, 1, 256), F32)
            if k == 0:
                total = jnp.concatenate([gap, total[:, :-1]], axis=1)
            elif k == 2:
                total = jnp.concatenate([total[:, 1:], gap], axis=1)
            else:
                kept = total[:, :, 192:256]
            tall = total if tall is None else tall + total
        gap = jnp.zeros((1, 8, 64), F32)
        total = (
            jnp.concatenate([gap, tall[:-1, :, 0:64]], axis=0)
            + tall[:, :, 64:128]
            + jnp.concatenate([tall[1:, :, 128:192], gap], axis=0)
        )
        moved[128 * n : 128 * n + 128, 0:64] = (kept + leaky_relu(total)).reshape(128, 64)
    total = None
    for h in range(8):
        rows = moved[pl.ds(h, 16 * count, stride=8), :].astype(BF)
        term = jnp.dot(rows[:, 0:64], spread_ref[h], preferred_element_type=F32)
        total = term if total is None else total + term
    return total.astype(BF)


def coarse_kernel_body(own_ref, near_ref, far_ref, halo_ref, last_ref, wc_ref, spread_ref, out_ref, slab, moved):
    band = lax.axis_index("blk")
    odd = 2 * jnp.bitwise_and(band, 1)
    for place, block in enumerate((own_ref[...], near_ref[...], far_ref[...], last_ref[0:160])):
        lay(slab, 2, jnp.bitwise_xor(band, place), block)
    halves = (halo_ref[0:80], halo_ref[80:160], last_ref[240:320], last_ref[160:240])
    for place, block in enumerate(halves):
        lay(slab, 0, jnp.bitwise_xor(jnp.bitwise_xor(band, place), odd), block)
    out_ref[...] = coarse_rows(slab, wc_ref, spread_ref, moved, 0, 4).reshape(4, 16, 512)


def moved_by(x, sectors, band_of):
    count, bands = lax.axis_size("sector"), lax.axis_size("blk")
    pairs = []
    for s in range(count):
        for b in range(bands):
            if 0 <= band_of(b) < bands:
                pairs.append((s * bands + b, (s + sectors) % count * bands + band_of(b)))
    return lax.ppermute(x, ("sector", "blk"), pairs)


def shaped(*dims, dtype=BF):
    return jax.ShapeDtypeStruct(dims, dtype)


def run(kernel, outs, scratch, flops, name, *args, limit=24, hbm=(), aliases=None):
    return pl.pallas_call(
        kernel,
        out_shape=outs,
        in_specs=[pl.BlockSpec(memory_space=pltpu.HBM) if n in hbm else VMEM for n in range(len(args))],
        out_specs=jax.tree.map(lambda _: VMEM, outs),
        scratch_shapes=scratch,
        input_output_aliases=aliases or {},
        compiler_params=pltpu.CompilerParams(vmem_limit_bytes=limit << 20),
        cost_estimate=pl.CostEstimate(flops=flops, bytes_accessed=min(flops, 1 << 20), transcendentals=0),
        name=name,
    )(*args)


def per_device(features, residual_first, residual_second, shortcut_first, shortcut_second,
               first_reduce_weight, second_reduce_weight, coarse_kernel):
    own_band = run(band_edge_kernel, shaped(16, EDGE, 16, 128), (), 2 << 30, "band_edge", features)
    band_edge = moved_by(own_band, 0, lambda b: b - 1)
    sector_edge, corner = run(
        sector_edge_kernel, (shaped(ROWS, 16, 16, 128), shaped(ROWS, EDGE, 16, 128)), (), 4 << 30,
        "sector_edge", features, own_band,
    )
    sector_edge = moved_by(sector_edge, -1, lambda b: b)
    corner = moved_by(corner, -1, lambda b: b - 1)
    held = (
        shaped(22, 22, 16, 256), shaped(21, 22, 16, 256), shaped(22, 20, 16, 256), shaped(21, 21, 16, 256),
        shaped(9, 11, 16, 128, dtype=F32),
    )
    made = run(
        inner_kernel,
        (shaped(4, 256, 256),) * 4 + (shaped(256, 512), shaped(256, 256), shaped(256, 256), shaped(256, 128)) + held,
        (
            pltpu.VMEM((14, 14, 16, 128), F32),
        ),
        6 << 30, "inner", features,
        residual_first, residual_second, shortcut_first, shortcut_second, first_reduce_weight,
    )
    weights, levels = made[:8], made[8:]
    levels = run(
        band_kernel, held, (pltpu.VMEM((14, 6, 16, 128), F32),),
        3 << 30, "band", *levels, band_edge, *weights,
        aliases={n: n for n in range(5)},
    )
    *levels, sector_edge, corner = lax.optimization_barrier((*levels, sector_edge, corner))
    y, *_ = run(
        outer_kernel,
        (shaped(160, 256),) + held,
        (pltpu.VMEM((2, 20, 16, 128), F32), pltpu.VMEM((9, 11, 8, 384), F32)),
        4 << 30, "outer", *levels, sector_edge, corner, *weights, second_reduce_weight,
        aliases={n: n + 1 for n in range(5)},
    )
    near = moved_by(y, 0, lambda b: b ^ 1)
    far = moved_by(y, 0, lambda b: b ^ 2)
    halo = moved_by(jnp.concatenate([y[80:160], near[80:160]], axis=0), 1, lambda b: b ^ 2 if b % 2 else b)
    wc, spread = run(
        late_kernel,
        (shaped(3, 3, 256, 256), shaped(8, 64, 512)),
        (), 4 << 30, "late", y, jnp.swapaxes(coarse_kernel, 3, 4), limit=8,
    )
    far, halo, wc, spread = lax.optimization_barrier((far, halo, wc, spread))
    last = moved_by(jnp.concatenate([far, halo], axis=0), 0, lambda b: b ^ 1)
    return run(
        coarse_kernel_body,
        shaped(4, 16, 512),
        (pltpu.VMEM((6, 18, 8, 256), F32), pltpu.VMEM((512, 128), F32)),
        2 << 30, "coarse", y, near, far, halo, last, wc, spread, limit=16,
    )


def solution(mesh):
    in_specs = (P("sector", "blk", None),) + (P(),) * 6 + (P(None, None, None, None, "blk"),)
    return jax.shard_map(
        per_device, mesh=mesh, in_specs=in_specs, out_specs=P("sector", None, "blk"), check_vma=False
    )
```

```python
import jax
import jax.numpy as jnp
from jax import lax
from jax.experimental import pallas as pl
from jax.experimental.pallas import tpu as pltpu
from jax.sharding import PartitionSpec as P

BF = jnp.bfloat16
F32 = jnp.float32
ROWS = 5
EDGE = 5
VMEM = pl.BlockSpec(memory_space=pltpu.VMEM)


def leaky_relu(values):
    return jnp.maximum(values, 0.01 * values)


def beside(tiles):
    gap = jnp.zeros(tiles.shape[:-2] + (1, tiles.shape[-1]), tiles.dtype)
    after = jnp.concatenate([tiles[..., 1:, :], gap], axis=-2)
    before = jnp.concatenate([gap, tiles[..., :-1, :]], axis=-2)
    lane = lax.broadcasted_iota(jnp.int32, tiles.shape, tiles.ndim - 1)
    return jnp.where(lane < 64, after, before)


def under(tiles):
    gap = jnp.zeros(tiles.shape[:-2] + (1, tiles.shape[-1]), tiles.dtype)
    return jnp.concatenate([gap, tiles[..., :-1, :]], axis=-2)


def put(ref, index, tiles, second=beside):
    ref[index + (slice(None), slice(0, 128))] = tiles
    ref[index + (slice(None), slice(128, 256))] = second(tiles)


def flat(tiles):
    return tiles.reshape(-1, tiles.shape[-1])


def spaced(ref, a, rows, a_step, r, cols, r_step):
    lines = []
    for n in range(rows):
        if r_step == 1:
            lines.append(ref[a + a_step * n, r : r + cols])
        else:
            lines.append(jnp.stack([ref[a + a_step * n, r + r_step * m] for m in range(cols)]))
    return jnp.stack(lines)


def pair_dot(source, weights):
    total = None
    for slot in range(4):
        term = jnp.dot(flat(source(slot)), weights[slot], preferred_element_type=F32)
        total = term if total is None else total + term
    return leaky_relu(total)


def along_a(source, weights, a, pairs, r, count):
    total = pair_dot(lambda s: spaced(source, a - 1 + s, pairs, 2, r, count, 1), weights)
    return total.reshape(pairs, count, 16, 256)


def along_r(source, weights, a, count, r, pairs):
    total = pair_dot(lambda s: spaced(source, a, count, 1, r + s, pairs, 2), weights)
    return total.reshape(count, pairs, 16, 256)


def fill_p(xx, pp, weights, a, pairs, r, count):
    for pair in range(pairs):
        for first in range(0, count, 8):
            width = min(8, count - first)
            total = along_a(xx, weights, a + 2 * pair, 1, r + 1 + first, width).astype(BF)[0]
            at = slice(r + 1 + first, r + 1 + first + width)
            for side in range(2):
                put(pp, (a + 2 * pair + side, at), total[:, :, 128 * side : 128 * side + 128])


def fill_q(xx, qq, weights, a, count, r, pairs, step):
    for first in range(a, a + count, step):
        rows = min(step, a + count - first)
        total = along_r(xx, weights, first, rows, r, pairs).astype(BF)
        for pair in range(pairs):
            for side in range(2):
                put(qq, (slice(first, first + rows), r + 2 * pair + side), total[:, pair, :, 128 * side : 128 * side + 128])


def fill_f(pp, qq, ff, part, wp, wq, a, a_pairs, r, r_pairs):
    count, span = 2 * a_pairs, 2 * r_pairs
    total = along_r(pp, wp, a, count, r, r_pairs)
    for pair in range(r_pairs):
        for side in range(2):
            part[0:count, 2 * pair + side] = total[:, pair, :, 128 * side : 128 * side + 128]
    total = along_a(qq, wq, a, a_pairs, r, span)
    for pair in range(a_pairs):
        for side in range(2):
            tiles = total[pair, :, :, 128 * side : 128 * side + 128] + part[2 * pair + side, 0:span]
            put(ff, (a + 2 * pair + side, slice(r + 1, r + 1 + span)), tiles.astype(BF), under)


def fill_g(ff, gg, w_oo, w_oe, w_eo, w_ee, a, rows, r, cols):
    def product(first_a, na, first_r, nr, weights):
        tiles = spaced(ff, first_a, na, 2, first_r + 1, nr, 2)
        total = jnp.dot(flat(tiles), weights[...], preferred_element_type=F32)
        return total.reshape(na, nr, 16, -1)

    odd = product(2 * a - 1, rows + 1, 2 * r - 1, cols + 1, w_oo)
    total = odd[:rows, :cols, :, 0:128] + odd[:rows, 1:, :, 128:256]
    total = total + (odd[1:, :cols, :, 256:384] + odd[1:, 1:, :, 384:512])
    mixed = product(2 * a - 1, rows + 1, 2 * r, cols, w_oe)
    total = total + (mixed[:rows, :, :, 0:128] + mixed[1:, :, :, 128:256])
    mixed = product(2 * a, rows, 2 * r - 1, cols + 1, w_eo)
    total = total + (mixed[:, :cols, :, 0:128] + mixed[:, 1:, :, 128:256])
    total = total + product(2 * a, rows, 2 * r, cols, w_ee)
    gg[a - 1 : a - 1 + rows, r + 1 : r + 1 + cols] = leaky_relu(total).astype(BF).astype(F32)


def sector_edge_kernel(x_ref, sector_ref):
    for a in range(ROWS):
        sector_ref[a] = x_ref[a].reshape(x_ref.shape[1], 16, 128)


def band_edge_kernel(x_ref, sector_ref, band_ref, corner_ref):
    for a in range(ROWS):
        corner_ref[a] = sector_ref[a, 0:EDGE]
        band_ref[a] = sector_ref[a, 0:EDGE]
    for a in range(ROWS, x_ref.shape[0]):
        band_ref[a] = x_ref[a, 0:8].reshape(8, 16, 128)[:EDGE]


def inner_kernel(
    x_ref, wp_raw, wp2_raw, wq_raw, wq2_raw, w1_raw,
    wp, wp2, wq, wq2, w_oo, w_oe, w_eo, w_ee, xx, pp, qq, ff, gg,
    part,
):
    own = x_ref.shape[0]
    blank = jnp.zeros((1, 16, 256), BF)
    for a in range(own + ROWS):
        xx[a, 0:1] = blank
        pp[a, 0:1] = blank
        ff[a, 0:1] = blank
    for a in range(9):
        gg[a, 0:1] = jnp.zeros((1, 16, 128), F32)
    xx[own + ROWS] = jnp.zeros(xx.shape[1:], BF)
    qq[own + ROWS] = jnp.zeros(qq.shape[1:], BF)
    for a in range(own):
        put(xx, (a, slice(1, own + 1)), x_ref[a].reshape(own, 16, 128))

    zero = jnp.zeros((64, 64), BF)
    for raw, out in ((wp_raw, wp), (wq_raw, wq), (wp2_raw, wp2), (wq2_raw, wq2)):
        for slot in range(4):
            for block, height in enumerate((0, 1, 2, -1)):
                for side in range(2):
                    tap = slot - side
                    parts = []
                    for upper in range(2):
                        k = height - upper + 1
                        inside = 0 <= tap <= 2 and 0 <= k <= 2
                        parts.append(raw[tap, k] if inside else zero)
                    out[slot, 64 * block : 64 * block + 64, 128 * side : 128 * side + 128] = (
                        jnp.concatenate(parts, axis=1)
                    )
    taps = (
        (w_oo, ((0, 0), (0, 2), (2, 0), (2, 2))), (w_oe, ((0, 1), (2, 1))), (w_eo, ((1, 0), (1, 2))), (w_ee, ((1, 1),)),
    )
    for out, pairs in taps:
        for n, (i, j) in enumerate(pairs):
            at = slice(128 * n, 128 * n + 128)
            out[0:64, at] = w1_raw[i, j, 1]
            out[64:128, at] = w1_raw[i, j, 2]
            out[128:192, at] = jnp.zeros((64, 128), BF)
            out[192:256, at] = w1_raw[i, j, 0]

    fill_p(xx, pp, wp, 1, 7, 0, 16)
    fill_q(xx, qq, wq, 0, 16, 0, 7, 2)
    for pair in range(7):
        fill_f(pp, qq, ff, part, wp2, wq2, 1 + 2 * pair, 1, 0, 7)
    fill_g(ff, gg, w_oo, w_oe, w_eo, w_ee, 1, 6, 0, 7)


def band_kernel(
    xx_in, pp_in, qq_in, ff_in, gg_in, band_ref,
    wp, wp2, wq, wq2, w_oo, w_oe, w_eo, w_ee,
    xx, pp, qq, ff, gg, part,
):
    own = band_ref.shape[0]
    for a in range(own):
        put(xx, (a, slice(own + 1, own + 1 + EDGE)), band_ref[a])
    total = along_a(xx, wp, 1, 7, 17, EDGE).astype(BF)
    for pair in range(7):
        for side in range(2):
            put(pp, (1 + 2 * pair + side, slice(17, 17 + EDGE)), total[pair, :, :, 128 * side : 128 * side + 128])
    fill_q(xx, qq, wq, 0, 16, 14, 3, 8)
    fill_f(pp, qq, ff, part, wp2, wq2, 1, 7, 14, 3)
    fill_g(ff, gg, w_oo, w_oe, w_eo, w_ee, 1, 6, 7, 3)


def outer_kernel(
    xx_in, pp_in, qq_in, ff_in, gg_in, sector_ref, corner_ref,
    wp, wp2, wq, wq2, w_oo, w_oe, w_eo, w_ee, w2_ref,
    y_ref, xx, pp, qq, ff, gg, part, cells,
):
    own = sector_ref.shape[1]
    for a in range(ROWS):
        put(xx, (own + a, slice(1, own + 1)), sector_ref[a])
        put(xx, (own + a, slice(own + 1, own + 1 + EDGE)), corner_ref[a])
    fill_p(xx, pp, wp, 15, 3, 0, 21)
    fill_q(xx, qq, wq, 16, 5, 0, 10, 1)
    for pair in range(3):
        fill_f(pp, qq, ff, part, wp2, wq2, 15 + 2 * pair, 1, 0, 10)
    fill_g(ff, gg, w_oo, w_oe, w_eo, w_ee, 7, 3, 0, 10)
    even = gg[:, :, pl.ds(0, 8, stride=2), :]
    odd = gg[:, :, pl.ds(1, 8, stride=2), :]
    cells[:, :, :, 0:128] = even
    cells[:, :, :, 128:256] = odd
    cells[:, :, :, 256:384] = under(odd)
    total = None
    for i in range(3):
        for j in range(3):
            rows = flat(spaced(cells, i, 4, 2, j, 5, 2)).astype(BF)
            term = jnp.dot(rows[:, 0:256], w2_ref[i, j, 1:3].reshape(256, 256), preferred_element_type=F32)
            term = term + jnp.dot(rows[:, 256:384], w2_ref[i, j, 0], preferred_element_type=F32)
            total = term if total is None else total + term
    y_ref[...] = leaky_relu(total).astype(BF)


def late_kernel(y_ref, raw, coarse_out, spread_out):
    row = lax.broadcasted_iota(jnp.int32, (64, 512), 0)
    col = lax.broadcasted_iota(jnp.int32, (64, 512), 1)
    for h in range(8):
        spread_out[h] = jnp.where(col == row * 8 + h, 1.0, 0.0).astype(BF)
    band = lax.axis_index("blk")
    row = lax.broadcasted_iota(jnp.int32, (64, 256), 0)
    col = lax.broadcasted_iota(jnp.int32, (64, 256), 1)
    own = jnp.where(col == row + 64 * band, 1.0, 0.0).astype(BF)
    for i in range(3):
        for k in range(3):
            last = own if i == 1 and k == 1 else jnp.zeros((64, 256), BF)
            coarse_out[i, k] = jnp.concatenate([raw[i, 0, k], raw[i, 1, k], raw[i, 2, k], last], axis=0).T


def lay(slab, first, other, block):
    block = block.astype(F32).reshape(-1, 5, 8, 256)
    at = slice(first, first + block.shape[0])
    slab[at, pl.ds(4 * other + 1, 4)] = block[:, 1:5]

    @pl.when(other == 0)
    def _():
        slab[at, 0:1] = block[:, 0:1]


def coarse_rows(slab, wc_ref, spread_ref, moved, first, count):
    cast = [slab[a, 0:16].astype(BF).reshape(128, 256) for a in range(first, first + count + 2)]
    for n in range(count):
        tall = None
        for k in range(3):
            total = None
            for i in range(3):
                term = jnp.dot(cast[n + i], wc_ref[i, k], preferred_element_type=F32)
                total = term if total is None else total + term
            total = total.reshape(16, 8, 256)
            gap = jnp.zeros((16, 1, 256), F32)
            if k == 0:
                total = jnp.concatenate([gap, total[:, :-1]], axis=1)
            elif k == 2:
                total = jnp.concatenate([total[:, 1:], gap], axis=1)
            else:
                kept = total[:, :, 192:256]
            tall = total if tall is None else tall + total
        gap = jnp.zeros((1, 8, 64), F32)
        total = (
            jnp.concatenate([gap, tall[:-1, :, 0:64]], axis=0)
            + tall[:, :, 64:128]
            + jnp.concatenate([tall[1:, :, 128:192], gap], axis=0)
        )
        moved[128 * n : 128 * n + 128, 0:64] = (kept + leaky_relu(total)).reshape(128, 64)
    total = None
    for h in range(8):
        rows = moved[pl.ds(h, 16 * count, stride=8), :].astype(BF)
        term = jnp.dot(rows[:, 0:64], spread_ref[h], preferred_element_type=F32)
        total = term if total is None else total + term
    return total.astype(BF)


def coarse_kernel_body(
    own_ref, near_ref, halo_ref, far_ref, far_halo_ref, last_ref, wc_ref, spread_ref, out_ref, slab, moved,
):
    band = lax.axis_index("blk")
    blocks = (
        (0, 2, own_ref[...]), (0, 0, halo_ref[...]), (1, 2, near_ref[...]), (1, 0, last_ref[0:80]),
        (2, 2, far_ref[...]), (2, 0, far_halo_ref[...]), (3, 2, last_ref[80:240]), (3, 0, last_ref[240:320]),
    )
    for place, first, block in blocks:
        lay(slab, first, jnp.bitwise_xor(band, place), block)
    out_ref[...] = coarse_rows(slab, wc_ref, spread_ref, moved, 0, 4).reshape(4, 16, 512)


def moved_by(x, sectors, band_of):
    count, bands = lax.axis_size("sector"), lax.axis_size("blk")
    pairs = []
    for s in range(count):
        for b in range(bands):
            if 0 <= band_of(b) < bands:
                pairs.append((s * bands + b, (s + sectors) % count * bands + band_of(b)))
    return lax.ppermute(x, ("sector", "blk"), pairs)


def shaped(*dims, dtype=BF):
    return jax.ShapeDtypeStruct(dims, dtype)


def run(kernel, outs, scratch, flops, name, *args, limit=24, hbm=(), aliases=None):
    return pl.pallas_call(
        kernel,
        out_shape=outs,
        in_specs=[pl.BlockSpec(memory_space=pltpu.HBM) if n in hbm else VMEM for n in range(len(args))],
        out_specs=jax.tree.map(lambda _: VMEM, outs),
        scratch_shapes=scratch,
        input_output_aliases=aliases or {},
        compiler_params=pltpu.CompilerParams(vmem_limit_bytes=limit << 20),
        cost_estimate=pl.CostEstimate(flops=flops, bytes_accessed=min(flops, 1 << 20), transcendentals=0),
        name=name,
    )(*args)


def per_device(features, residual_first, residual_second, shortcut_first, shortcut_second,
               first_reduce_weight, second_reduce_weight, coarse_kernel):
    own_sector = run(sector_edge_kernel, shaped(ROWS, 16, 16, 128), (), 2 << 30, "sector_edge", features)
    sector_edge = moved_by(own_sector, -1, lambda b: b)
    band_edge, corner = run(
        band_edge_kernel, (shaped(16, EDGE, 16, 128), shaped(ROWS, EDGE, 16, 128)), (), 4 << 30, "band_edge", features, own_sector
    )
    band_edge = moved_by(band_edge, 0, lambda b: b - 1)
    corner = moved_by(corner, -1, lambda b: b - 1)
    held = (
        shaped(22, 22, 16, 256), shaped(21, 22, 16, 256), shaped(22, 20, 16, 256), shaped(21, 21, 16, 256),
        shaped(9, 11, 16, 128, dtype=F32),
    )
    made = run(
        inner_kernel,
        (shaped(4, 256, 256),) * 4 + (shaped(256, 512), shaped(256, 256), shaped(256, 256), shaped(256, 128)) + held,
        (
            pltpu.VMEM((14, 14, 16, 128), F32),
        ),
        1 << 20, "inner", features,
        residual_first, residual_second, shortcut_first, shortcut_second, first_reduce_weight,
    )
    weights, levels = made[:8], made[8:]
    levels = run(
        band_kernel, held, (pltpu.VMEM((14, 6, 16, 128), F32),),
        1 << 20, "band", *levels, band_edge, *weights,
        aliases={n: n for n in range(5)},
    )
    *levels, sector_edge, corner = lax.optimization_barrier((*levels, sector_edge, corner))
    y, *_ = run(
        outer_kernel,
        (shaped(160, 256),) + held,
        (pltpu.VMEM((2, 20, 16, 128), F32), pltpu.VMEM((9, 11, 8, 384), F32)),
        4 << 30, "outer", *levels, sector_edge, corner, *weights, second_reduce_weight,
        aliases={n: n + 1 for n in range(5)},
    )
    halo = moved_by(y[80:160], 1, lambda b: b)
    far_halo = moved_by(y[80:160], 1, lambda b: b ^ 2)
    far = moved_by(y, 0, lambda b: b ^ 2)
    near = moved_by(y, 0, lambda b: b ^ 1)
    wc, spread = run(
        late_kernel,
        (shaped(3, 3, 256, 256), shaped(8, 64, 512)),
        (), 4 << 30, "late", y, jnp.swapaxes(coarse_kernel, 3, 4), limit=8,
    )
    halo, far_halo, far, near, wc, spread = lax.optimization_barrier((halo, far_halo, far, near, wc, spread))
    last = moved_by(jnp.concatenate([halo, far, far_halo], axis=0), 0, lambda b: b ^ 1)
    return run(
        coarse_kernel_body,
        shaped(4, 16, 512),
        (pltpu.VMEM((6, 18, 8, 256), F32), pltpu.VMEM((512, 128), F32)),
        2 << 30, "coarse", y, near, halo, far, far_halo, last, wc, spread, limit=16,
    )


def solution(mesh):
    in_specs = (P("sector", "blk", None),) + (P(),) * 6 + (P(None, None, None, None, "blk"),)
    return jax.shard_map(
        per_device, mesh=mesh, in_specs=in_specs, out_specs=P("sector", None, "blk"), check_vma=False
    )
```

```python
import jax
import jax.numpy as jnp
from jax import lax
from jax.experimental import pallas as pl
from jax.experimental.pallas import tpu as pltpu
from jax.sharding import PartitionSpec as P

BF = jnp.bfloat16
F32 = jnp.float32
ROWS = 5
EDGE = 5
VMEM = pl.BlockSpec(memory_space=pltpu.VMEM)


def leaky_relu(values):
    return jnp.maximum(values, 0.01 * values)


def beside(tiles):
    gap = jnp.zeros(tiles.shape[:-2] + (1, tiles.shape[-1]), tiles.dtype)
    after = jnp.concatenate([tiles[..., 1:, :], gap], axis=-2)
    before = jnp.concatenate([gap, tiles[..., :-1, :]], axis=-2)
    lane = lax.broadcasted_iota(jnp.int32, tiles.shape, tiles.ndim - 1)
    return jnp.where(lane < 64, after, before)


def under(tiles):
    gap = jnp.zeros(tiles.shape[:-2] + (1, tiles.shape[-1]), tiles.dtype)
    return jnp.concatenate([gap, tiles[..., :-1, :]], axis=-2)


def put(ref, index, tiles, second=beside):
    ref[index + (slice(None), slice(0, 128))] = tiles
    ref[index + (slice(None), slice(128, 256))] = second(tiles)


def flat(tiles):
    return tiles.reshape(-1, tiles.shape[-1])


def spaced(ref, a, rows, a_step, r, cols, r_step):
    lines = []
    for n in range(rows):
        if r_step == 1:
            lines.append(ref[a + a_step * n, r : r + cols])
        else:
            lines.append(jnp.stack([ref[a + a_step * n, r + r_step * m] for m in range(cols)]))
    return jnp.stack(lines)


def pair_dot(source, weights):
    total = None
    for slot in range(4):
        term = jnp.dot(flat(source(slot)), weights[slot], preferred_element_type=F32)
        total = term if total is None else total + term
    return leaky_relu(total)


def along_a(source, weights, a, pairs, r, count):
    total = pair_dot(lambda s: spaced(source, a - 1 + s, pairs, 2, r, count, 1), weights)
    return total.reshape(pairs, count, 16, 256)


def along_r(source, weights, a, count, r, pairs):
    total = pair_dot(lambda s: spaced(source, a, count, 1, r + s, pairs, 2), weights)
    return total.reshape(count, pairs, 16, 256)


def fill_p(xx, pp, weights, a, pairs, r, count):
    for pair in range(pairs):
        for first in range(0, count, 8):
            width = min(8, count - first)
            total = along_a(xx, weights, a + 2 * pair, 1, r + 1 + first, width).astype(BF)[0]
            at = slice(r + 1 + first, r + 1 + first + width)
            for side in range(2):
                put(pp, (a + 2 * pair + side, at), total[:, :, 128 * side : 128 * side + 128])


def fill_q(xx, qq, weights, a, count, r, pairs, step):
    for first in range(a, a + count, step):
        rows = min(step, a + count - first)
        total = along_r(xx, weights, first, rows, r, pairs).astype(BF)
        for pair in range(pairs):
            for side in range(2):
                put(qq, (slice(first, first + rows), r + 2 * pair + side), total[:, pair, :, 128 * side : 128 * side + 128])


def fill_f(pp, qq, ff, part, wp, wq, a, a_pairs, r, r_pairs):
    count, span = 2 * a_pairs, 2 * r_pairs
    total = along_r(pp, wp, a, count, r, r_pairs)
    for pair in range(r_pairs):
        for side in range(2):
            part[0:count, 2 * pair + side] = total[:, pair, :, 128 * side : 128 * side + 128]
    total = along_a(qq, wq, a, a_pairs, r, span)
    for pair in range(a_pairs):
        for side in range(2):
            tiles = total[pair, :, :, 128 * side : 128 * side + 128] + part[2 * pair + side, 0:span]
            put(ff, (a + 2 * pair + side, slice(r + 1, r + 1 + span)), tiles.astype(BF), under)


def fill_g(ff, gg, w_oo, w_oe, w_eo, w_ee, a, rows, r, cols):
    def product(first_a, na, first_r, nr, weights):
        tiles = spaced(ff, first_a, na, 2, first_r + 1, nr, 2)
        total = jnp.dot(flat(tiles), weights[...], preferred_element_type=F32)
        return total.reshape(na, nr, 16, -1)

    odd = product(2 * a - 1, rows + 1, 2 * r - 1, cols + 1, w_oo)
    total = odd[:rows, :cols, :, 0:128] + odd[:rows, 1:, :, 128:256]
    total = total + (odd[1:, :cols, :, 256:384] + odd[1:, 1:, :, 384:512])
    mixed = product(2 * a - 1, rows + 1, 2 * r, cols, w_oe)
    total = total + (mixed[:rows, :, :, 0:128] + mixed[1:, :, :, 128:256])
    mixed = product(2 * a, rows, 2 * r - 1, cols + 1, w_eo)
    total = total + (mixed[:, :cols, :, 0:128] + mixed[:, 1:, :, 128:256])
    total = total + product(2 * a, rows, 2 * r, cols, w_ee)
    gg[a - 1 : a - 1 + rows, r + 1 : r + 1 + cols] = leaky_relu(total).astype(BF).astype(F32)


def sector_edge_kernel(x_ref, sector_ref, corner_ref):
    for a in range(ROWS):
        tiles = x_ref[a].reshape(x_ref.shape[1], 16, 128)
        sector_ref[a] = tiles
        corner_ref[a] = tiles[:EDGE]


def band_edge_kernel(x_ref, corner_ref, band_ref):
    band_ref[0:ROWS] = corner_ref[...]
    for a in range(ROWS, x_ref.shape[0]):
        band_ref[a] = x_ref[a].reshape(8, 16, 128)[:EDGE]


def inner_kernel(
    x_ref, wp_raw, wp2_raw, wq_raw, wq2_raw, w1_raw,
    wp, wp2, wq, wq2, w_oo, w_oe, w_eo, w_ee, xx, pp, qq, ff, gg,
    part,
):
    own = x_ref.shape[0]
    blank = jnp.zeros((1, 16, 256), BF)
    for a in range(own + ROWS):
        xx[a, 0:1] = blank
        pp[a, 0:1] = blank
        ff[a, 0:1] = blank
    for a in range(9):
        gg[a, 0:1] = jnp.zeros((1, 16, 128), F32)
    xx[own + ROWS] = jnp.zeros(xx.shape[1:], BF)
    qq[own + ROWS] = jnp.zeros(qq.shape[1:], BF)
    for a in range(own):
        put(xx, (a, slice(1, own + 1)), x_ref[a].reshape(own, 16, 128))

    zero = jnp.zeros((64, 64), BF)
    for raw, out in ((wp_raw, wp), (wq_raw, wq), (wp2_raw, wp2), (wq2_raw, wq2)):
        for slot in range(4):
            for block, height in enumerate((0, 1, 2, -1)):
                for side in range(2):
                    tap = slot - side
                    parts = []
                    for upper in range(2):
                        k = height - upper + 1
                        inside = 0 <= tap <= 2 and 0 <= k <= 2
                        parts.append(raw[tap, k] if inside else zero)
                    out[slot, 64 * block : 64 * block + 64, 128 * side : 128 * side + 128] = (
                        jnp.concatenate(parts, axis=1)
                    )
    taps = (
        (w_oo, ((0, 0), (0, 2), (2, 0), (2, 2))), (w_oe, ((0, 1), (2, 1))), (w_eo, ((1, 0), (1, 2))), (w_ee, ((1, 1),)),
    )
    for out, pairs in taps:
        for n, (i, j) in enumerate(pairs):
            at = slice(128 * n, 128 * n + 128)
            out[0:64, at] = w1_raw[i, j, 1]
            out[64:128, at] = w1_raw[i, j, 2]
            out[128:192, at] = jnp.zeros((64, 128), BF)
            out[192:256, at] = w1_raw[i, j, 0]

    fill_p(xx, pp, wp, 1, 7, 0, 16)
    fill_q(xx, qq, wq, 0, 16, 0, 7, 2)
    for pair in range(7):
        fill_f(pp, qq, ff, part, wp2, wq2, 1 + 2 * pair, 1, 0, 7)
    fill_g(ff, gg, w_oo, w_oe, w_eo, w_ee, 1, 6, 0, 7)


def rows_kernel(
    xx_in, pp_in, qq_in, ff_in, gg_in, sector_ref,
    wp, wp2, wq, wq2, w_oo, w_oe, w_eo, w_ee,
    xx, pp, qq, ff, gg, part,
):
    own = sector_ref.shape[1]
    for a in range(ROWS):
        put(xx, (own + a, slice(1, own + 1)), sector_ref[a])
    fill_p(xx, pp, wp, 15, 3, 0, 16)
    fill_q(xx, qq, wq, 16, 5, 0, 7, 1)
    for pair in range(3):
        fill_f(pp, qq, ff, part, wp2, wq2, 15 + 2 * pair, 1, 0, 7)
    fill_g(ff, gg, w_oo, w_oe, w_eo, w_ee, 7, 3, 0, 7)


def columns_kernel(
    xx_in, pp_in, qq_in, ff_in, gg_in, band_ref, corner_ref,
    wp, wp2, wq, wq2, w_oo, w_oe, w_eo, w_ee, w2_ref,
    y_ref, xx, pp, qq, ff, gg, part, cells,
):
    own = band_ref.shape[0]
    for a in range(own):
        put(xx, (a, slice(own + 1, own + 1 + EDGE)), band_ref[a])
    for a in range(ROWS):
        put(xx, (own + a, slice(own + 1, own + 1 + EDGE)), corner_ref[a])
    for first in (1, 11):
        total = along_a(xx, wp, first, 5, 17, EDGE).astype(BF)
        for pair in range(5):
            for side in range(2):
                tiles = total[pair, :, :, 128 * side : 128 * side + 128]
                put(pp, (first + 2 * pair + side, slice(17, 17 + EDGE)), tiles)
    fill_q(xx, qq, wq, 0, 21, 14, 3, 7)
    for first in (1, 11):
        fill_f(pp, qq, ff, part, wp2, wq2, first, 5, 14, 3)
    fill_g(ff, gg, w_oo, w_oe, w_eo, w_ee, 1, 9, 7, 3)

    even = gg[:, :, pl.ds(0, 8, stride=2), :]
    odd = gg[:, :, pl.ds(1, 8, stride=2), :]
    cells[:, :, :, 0:128] = even
    cells[:, :, :, 128:256] = odd
    cells[:, :, :, 256:384] = under(odd)
    total = None
    for i in range(3):
        for j in range(3):
            rows = flat(spaced(cells, i, 4, 2, j, 5, 2)).astype(BF)
            term = jnp.dot(rows[:, 0:256], w2_ref[i, j, 1:3].reshape(256, 256), preferred_element_type=F32)
            term = term + jnp.dot(rows[:, 256:384], w2_ref[i, j, 0], preferred_element_type=F32)
            total = term if total is None else total + term
    y_ref[...] = leaky_relu(total).astype(BF)


def late_kernel(y_ref, raw, coarse_out, spread_out):
    row = lax.broadcasted_iota(jnp.int32, (64, 512), 0)
    col = lax.broadcasted_iota(jnp.int32, (64, 512), 1)
    for h in range(8):
        spread_out[h] = jnp.where(col == row * 8 + h, 1.0, 0.0).astype(BF)
    band = lax.axis_index("blk")
    row = lax.broadcasted_iota(jnp.int32, (64, 256), 0)
    col = lax.broadcasted_iota(jnp.int32, (64, 256), 1)
    own = jnp.where(col == row + 64 * band, 1.0, 0.0).astype(BF)
    for i in range(3):
        for k in range(3):
            last = own if i == 1 and k == 1 else jnp.zeros((64, 256), BF)
            coarse_out[i, k] = jnp.concatenate([raw[i, 0, k], raw[i, 1, k], raw[i, 2, k], last], axis=0).T


def lay(slab, first, other, block):
    block = block.astype(F32).reshape(-1, 5, 8, 256)
    at = slice(first, first + block.shape[0])
    slab[at, pl.ds(4 * other + 1, 4)] = block[:, 1:5]

    @pl.when(other == 0)
    def _():
        slab[at, 0:1] = block[:, 0:1]


def coarse_rows(slab, wc_ref, spread_ref, moved, first, count):
    cast = [slab[a, 0:16].astype(BF).reshape(128, 256) for a in range(first, first + count + 2)]
    for n in range(count):
        tall = None
        for k in range(3):
            total = None
            for i in range(3):
                term = jnp.dot(cast[n + i], wc_ref[i, k], preferred_element_type=F32)
                total = term if total is None else total + term
            total = total.reshape(16, 8, 256)
            gap = jnp.zeros((16, 1, 256), F32)
            if k == 0:
                total = jnp.concatenate([gap, total[:, :-1]], axis=1)
            elif k == 2:
                total = jnp.concatenate([total[:, 1:], gap], axis=1)
            else:
                kept = total[:, :, 192:256]
            tall = total if tall is None else tall + total
        gap = jnp.zeros((1, 8, 64), F32)
        total = (
            jnp.concatenate([gap, tall[:-1, :, 0:64]], axis=0)
            + tall[:, :, 64:128]
            + jnp.concatenate([tall[1:, :, 128:192], gap], axis=0)
        )
        moved[128 * n : 128 * n + 128, 0:64] = (kept + leaky_relu(total)).reshape(128, 64)
    total = None
    for h in range(8):
        rows = moved[pl.ds(h, 16 * count, stride=8), :].astype(BF)
        term = jnp.dot(rows[:, 0:64], spread_ref[h], preferred_element_type=F32)
        total = term if total is None else total + term
    return total.astype(BF)


def coarse_kernel_body(
    own_ref, near_ref, halo_ref, far_ref, far_halo_ref, last_ref, wc_ref, spread_ref, out_ref, slab, moved,
):
    band = lax.axis_index("blk")
    blocks = (
        (0, 2, own_ref[...]), (0, 0, halo_ref[...]), (1, 2, near_ref[...]), (1, 0, last_ref[0:80]),
        (2, 2, far_ref[...]), (2, 0, far_halo_ref[...]), (3, 2, last_ref[80:240]), (3, 0, last_ref[240:320]),
    )
    for place, first, block in blocks:
        lay(slab, first, jnp.bitwise_xor(band, place), block)
    out_ref[...] = coarse_rows(slab, wc_ref, spread_ref, moved, 0, 4).reshape(4, 16, 512)


def moved_by(x, sectors, band_of):
    count, bands = lax.axis_size("sector"), lax.axis_size("blk")
    pairs = []
    for s in range(count):
        for b in range(bands):
            if 0 <= band_of(b) < bands:
                pairs.append((s * bands + b, (s + sectors) % count * bands + band_of(b)))
    return lax.ppermute(x, ("sector", "blk"), pairs)


def shaped(*dims, dtype=BF):
    return jax.ShapeDtypeStruct(dims, dtype)


def run(kernel, outs, scratch, flops, name, *args, limit=24, hbm=(), aliases=None):
    return pl.pallas_call(
        kernel,
        out_shape=outs,
        in_specs=[pl.BlockSpec(memory_space=pltpu.HBM) if n in hbm else VMEM for n in range(len(args))],
        out_specs=jax.tree.map(lambda _: VMEM, outs),
        scratch_shapes=scratch,
        input_output_aliases=aliases or {},
        compiler_params=pltpu.CompilerParams(vmem_limit_bytes=limit << 20),
        cost_estimate=pl.CostEstimate(flops=flops, bytes_accessed=min(flops, 1 << 20), transcendentals=0),
        name=name,
    )(*args)


def per_device(features, residual_first, residual_second, shortcut_first, shortcut_second,
               first_reduce_weight, second_reduce_weight, coarse_kernel):
    sector_edge, corner = run(
        sector_edge_kernel, (shaped(ROWS, 16, 16, 128), shaped(ROWS, EDGE, 16, 128)), (), 2 << 30, "sector_edge", features[0:ROWS]
    )
    band_edge = run(band_edge_kernel, shaped(16, EDGE, 16, 128), (), 4 << 30, "band_edge", features[:, 0:8], corner)
    sector_edge = moved_by(sector_edge, -1, lambda b: b)
    band_edge = moved_by(band_edge, 0, lambda b: b - 1)
    corner = moved_by(corner, -1, lambda b: b - 1)
    held = (
        shaped(22, 22, 16, 256), shaped(21, 22, 16, 256), shaped(22, 20, 16, 256), shaped(21, 21, 16, 256),
        shaped(9, 11, 16, 128, dtype=F32),
    )
    made = run(
        inner_kernel,
        (shaped(4, 256, 256),) * 4 + (shaped(256, 512), shaped(256, 256), shaped(256, 256), shaped(256, 128)) + held,
        (
            pltpu.VMEM((14, 14, 16, 128), F32),
        ),
        1 << 20, "inner", features,
        residual_first, residual_second, shortcut_first, shortcut_second, first_reduce_weight,
    )
    weights, levels = made[:8], made[8:]
    levels = run(
        rows_kernel, held, (pltpu.VMEM((2, 14, 16, 128), F32),),
        1 << 20, "rows", *levels, sector_edge, *weights,
        aliases={n: n for n in range(5)},
    )
    *levels, band_edge, corner = lax.optimization_barrier((*levels, band_edge, corner))
    y, *_ = run(
        columns_kernel,
        (shaped(160, 256),) + held,
        (pltpu.VMEM((10, 6, 16, 128), F32), pltpu.VMEM((9, 11, 8, 384), F32)),
        4 << 30, "columns", *levels, band_edge, corner, *weights, second_reduce_weight,
        aliases={n: n + 1 for n in range(5)},
    )
    halo = moved_by(y[80:160], 1, lambda b: b)
    far_halo = moved_by(y[80:160], 1, lambda b: b ^ 2)
    far = moved_by(y, 0, lambda b: b ^ 2)
    near = moved_by(y, 0, lambda b: b ^ 1)
    wc, spread = run(
        late_kernel,
        (shaped(3, 3, 256, 256), shaped(8, 64, 512)),
        (), 4 << 30, "late", y, jnp.swapaxes(coarse_kernel, 3, 4), limit=8,
    )
    halo, far_halo, far, near, wc, spread = lax.optimization_barrier((halo, far_halo, far, near, wc, spread))
    last = moved_by(jnp.concatenate([halo, far, far_halo], axis=0), 0, lambda b: b ^ 1)
    return run(
        coarse_kernel_body,
        shaped(4, 16, 512),
        (pltpu.VMEM((6, 18, 8, 256), F32), pltpu.VMEM((512, 128), F32)),
        2 << 30, "coarse", y, near, halo, far, far_halo, last, wc, spread, limit=16,
    )


def solution(mesh):
    in_specs = (P("sector", "blk", None),) + (P(),) * 6 + (P(None, None, None, None, "blk"),)
    return jax.shard_map(
        per_device, mesh=mesh, in_specs=in_specs, out_specs=P("sector", None, "blk"), check_vma=False
    )
```

```python
import jax
import jax.numpy as jnp
from jax import lax
from jax.experimental import pallas as pl
from jax.experimental.pallas import tpu as pltpu
from jax.sharding import PartitionSpec as P

BF = jnp.bfloat16
F32 = jnp.float32
ROWS = 5
EDGE = 5
VMEM = pl.BlockSpec(memory_space=pltpu.VMEM)


def leaky_relu(values):
    return jnp.maximum(values, 0.01 * values)


def beside(tiles):
    gap = jnp.zeros(tiles.shape[:-2] + (1, tiles.shape[-1]), tiles.dtype)
    after = jnp.concatenate([tiles[..., 1:, :], gap], axis=-2)
    before = jnp.concatenate([gap, tiles[..., :-1, :]], axis=-2)
    lane = lax.broadcasted_iota(jnp.int32, tiles.shape, tiles.ndim - 1)
    return jnp.where(lane < 64, after, before)


def under(tiles):
    gap = jnp.zeros(tiles.shape[:-2] + (1, tiles.shape[-1]), tiles.dtype)
    return jnp.concatenate([gap, tiles[..., :-1, :]], axis=-2)


def put(ref, index, tiles, second=beside):
    ref[index + (slice(None), slice(0, 128))] = tiles
    ref[index + (slice(None), slice(128, 256))] = second(tiles)


def flat(tiles):
    return tiles.reshape(-1, tiles.shape[-1])


def spaced(ref, a, rows, a_step, r, cols, r_step):
    lines = []
    for n in range(rows):
        if r_step == 1:
            lines.append(ref[a + a_step * n, r : r + cols])
        else:
            lines.append(jnp.stack([ref[a + a_step * n, r + r_step * m] for m in range(cols)]))
    return jnp.stack(lines)


def pair_dot(source, weights):
    total = None
    for slot in range(4):
        term = jnp.dot(flat(source(slot)), weights[slot], preferred_element_type=F32)
        total = term if total is None else total + term
    return leaky_relu(total)


def along_a(source, weights, a, pairs, r, count):
    total = pair_dot(lambda s: spaced(source, a - 1 + s, pairs, 2, r, count, 1), weights)
    return total.reshape(pairs, count, 16, 256)


def along_r(source, weights, a, count, r, pairs):
    total = pair_dot(lambda s: spaced(source, a, count, 1, r + s, pairs, 2), weights)
    return total.reshape(count, pairs, 16, 256)


def fill_p(xx, pp, weights, a, pairs, r, count):
    for pair in range(pairs):
        for first in range(0, count, 8):
            width = min(8, count - first)
            total = along_a(xx, weights, a + 2 * pair, 1, r + 1 + first, width).astype(BF)[0]
            at = slice(r + 1 + first, r + 1 + first + width)
            for side in range(2):
                put(pp, (a + 2 * pair + side, at), total[:, :, 128 * side : 128 * side + 128])


def fill_q(xx, qq, weights, a, count, r, pairs, step):
    for first in range(a, a + count, step):
        rows = min(step, a + count - first)
        total = along_r(xx, weights, first, rows, r, pairs).astype(BF)
        for pair in range(pairs):
            for side in range(2):
                put(qq, (slice(first, first + rows), r + 2 * pair + side), total[:, pair, :, 128 * side : 128 * side + 128])


def fill_f(pp, qq, ff, part, wp, wq, a, a_pairs, r, r_pairs):
    count, span = 2 * a_pairs, 2 * r_pairs
    total = along_r(pp, wp, a, count, r, r_pairs)
    for pair in range(r_pairs):
        for side in range(2):
            part[0:count, 2 * pair + side] = total[:, pair, :, 128 * side : 128 * side + 128]
    total = along_a(qq, wq, a, a_pairs, r, span)
    for pair in range(a_pairs):
        for side in range(2):
            tiles = total[pair, :, :, 128 * side : 128 * side + 128] + part[2 * pair + side, 0:span]
            put(ff, (a + 2 * pair + side, slice(r + 1, r + 1 + span)), tiles.astype(BF), under)


def fill_g(ff, gg, w_oo, w_oe, w_eo, w_ee, a, rows, r, cols):
    def product(first_a, na, first_r, nr, weights):
        tiles = spaced(ff, first_a, na, 2, first_r + 1, nr, 2)
        total = jnp.dot(flat(tiles), weights[...], preferred_element_type=F32)
        return total.reshape(na, nr, 16, -1)

    odd = product(2 * a - 1, rows + 1, 2 * r - 1, cols + 1, w_oo)
    total = odd[:rows, :cols, :, 0:128] + odd[:rows, 1:, :, 128:256]
    total = total + (odd[1:, :cols, :, 256:384] + odd[1:, 1:, :, 384:512])
    mixed = product(2 * a - 1, rows + 1, 2 * r, cols, w_oe)
    total = total + (mixed[:rows, :, :, 0:128] + mixed[1:, :, :, 128:256])
    mixed = product(2 * a, rows, 2 * r - 1, cols + 1, w_eo)
    total = total + (mixed[:, :cols, :, 0:128] + mixed[:, 1:, :, 128:256])
    total = total + product(2 * a, rows, 2 * r, cols, w_ee)
    gg[a - 1 : a - 1 + rows, r + 1 : r + 1 + cols] = leaky_relu(total).astype(BF).astype(F32)


def sector_edge_kernel(x_ref, sector_ref, corner_ref):
    for a in range(ROWS):
        tiles = x_ref[a].reshape(x_ref.shape[1], 16, 128)
        sector_ref[a] = tiles
        corner_ref[a] = tiles[:EDGE]


def band_edge_kernel(x_ref, corner_ref, band_ref):
    band_ref[0:ROWS] = corner_ref[...]
    for a in range(ROWS, x_ref.shape[0]):
        band_ref[a] = x_ref[a].reshape(8, 16, 128)[:EDGE]


def inner_kernel(
    x_ref, wp_raw, wp2_raw, wq_raw, wq2_raw, w1_raw,
    wp, wp2, wq, wq2, w_oo, w_oe, w_eo, w_ee, xx, pp, qq, ff, gg,
    part,
):
    own = x_ref.shape[0]
    blank = jnp.zeros((1, 16, 256), BF)
    for a in range(own + ROWS):
        xx[a, 0:1] = blank
        pp[a, 0:1] = blank
        ff[a, 0:1] = blank
    for a in range(9):
        gg[a, 0:1] = jnp.zeros((1, 16, 128), F32)
    xx[own + ROWS] = jnp.zeros(xx.shape[1:], BF)
    qq[own + ROWS] = jnp.zeros(qq.shape[1:], BF)
    for a in range(own):
        put(xx, (a, slice(1, own + 1)), x_ref[a].reshape(own, 16, 128))

    zero = jnp.zeros((64, 64), BF)
    for raw, out in ((wp_raw, wp), (wq_raw, wq), (wp2_raw, wp2), (wq2_raw, wq2)):
        for slot in range(4):
            for block, height in enumerate((0, 1, 2, -1)):
                for side in range(2):
                    tap = slot - side
                    parts = []
                    for upper in range(2):
                        k = height - upper + 1
                        inside = 0 <= tap <= 2 and 0 <= k <= 2
                        parts.append(raw[tap, k] if inside else zero)
                    out[slot, 64 * block : 64 * block + 64, 128 * side : 128 * side + 128] = (
                        jnp.concatenate(parts, axis=1)
                    )
    taps = (
        (w_oo, ((0, 0), (0, 2), (2, 0), (2, 2))), (w_oe, ((0, 1), (2, 1))), (w_eo, ((1, 0), (1, 2))), (w_ee, ((1, 1),)),
    )
    for out, pairs in taps:
        for n, (i, j) in enumerate(pairs):
            at = slice(128 * n, 128 * n + 128)
            out[0:64, at] = w1_raw[i, j, 1]
            out[64:128, at] = w1_raw[i, j, 2]
            out[128:192, at] = jnp.zeros((64, 128), BF)
            out[192:256, at] = w1_raw[i, j, 0]

    fill_p(xx, pp, wp, 1, 7, 0, 16)
    fill_q(xx, qq, wq, 0, 16, 0, 7, 1)
    for pair in range(7):
        fill_f(pp, qq, ff, part, wp2, wq2, 1 + 2 * pair, 1, 0, 7)
    fill_g(ff, gg, w_oo, w_oe, w_eo, w_ee, 1, 6, 0, 7)


def rows_kernel(
    xx_in, pp_in, qq_in, ff_in, gg_in, sector_ref,
    wp, wp2, wq, wq2, w_oo, w_oe, w_eo, w_ee,
    xx, pp, qq, ff, gg, part,
):
    own = sector_ref.shape[1]
    for a in range(ROWS):
        put(xx, (own + a, slice(1, own + 1)), sector_ref[a])
    fill_p(xx, pp, wp, 15, 3, 0, 16)
    fill_q(xx, qq, wq, 16, 5, 0, 7, 1)
    for pair in range(3):
        fill_f(pp, qq, ff, part, wp2, wq2, 15 + 2 * pair, 1, 0, 7)
    fill_g(ff, gg, w_oo, w_oe, w_eo, w_ee, 7, 3, 0, 7)


def columns_kernel(
    xx_in, pp_in, qq_in, ff_in, gg_in, band_ref, corner_ref,
    wp, wp2, wq, wq2, w_oo, w_oe, w_eo, w_ee, w2_ref,
    y_ref, xx, pp, qq, ff, gg, part, cells,
):
    own = band_ref.shape[0]
    for a in range(own):
        put(xx, (a, slice(own + 1, own + 1 + EDGE)), band_ref[a])
    for a in range(ROWS):
        put(xx, (own + a, slice(own + 1, own + 1 + EDGE)), corner_ref[a])
    for first in (1, 11):
        total = along_a(xx, wp, first, 5, 17, EDGE).astype(BF)
        for pair in range(5):
            for side in range(2):
                tiles = total[pair, :, :, 128 * side : 128 * side + 128]
                put(pp, (first + 2 * pair + side, slice(17, 17 + EDGE)), tiles)
    fill_q(xx, qq, wq, 0, 21, 14, 3, 7)
    for first in (1, 11):
        fill_f(pp, qq, ff, part, wp2, wq2, first, 5, 14, 3)
    fill_g(ff, gg, w_oo, w_oe, w_eo, w_ee, 1, 9, 7, 3)

    even = gg[:, :, pl.ds(0, 8, stride=2), :]
    odd = gg[:, :, pl.ds(1, 8, stride=2), :]
    cells[:, :, :, 0:128] = even
    cells[:, :, :, 128:256] = odd
    cells[:, :, :, 256:384] = under(odd)
    total = None
    for i in range(3):
        for j in range(3):
            rows = flat(spaced(cells, i, 4, 2, j, 5, 2)).astype(BF)
            term = jnp.dot(rows[:, 0:256], w2_ref[i, j, 1:3].reshape(256, 256), preferred_element_type=F32)
            term = term + jnp.dot(rows[:, 256:384], w2_ref[i, j, 0], preferred_element_type=F32)
            total = term if total is None else total + term
    y_ref[...] = leaky_relu(total).astype(BF)


def late_kernel(y_ref, raw, coarse_out, spread_out):
    row = lax.broadcasted_iota(jnp.int32, (64, 512), 0)
    col = lax.broadcasted_iota(jnp.int32, (64, 512), 1)
    for h in range(8):
        spread_out[h] = jnp.where(col == row * 8 + h, 1.0, 0.0).astype(BF)
    band = lax.axis_index("blk")
    row = lax.broadcasted_iota(jnp.int32, (64, 256), 0)
    col = lax.broadcasted_iota(jnp.int32, (64, 256), 1)
    own = jnp.where(col == row + 64 * band, 1.0, 0.0).astype(BF)
    for i in range(3):
        for k in range(3):
            last = own if i == 1 and k == 1 else jnp.zeros((64, 256), BF)
            coarse_out[i, k] = jnp.concatenate([raw[i, 0, k], raw[i, 1, k], raw[i, 2, k], last], axis=0).T


def lay(slab, first, other, block):
    block = block.astype(F32).reshape(-1, 5, 8, 256)
    at = slice(first, first + block.shape[0])
    slab[at, pl.ds(4 * other + 1, 4)] = block[:, 1:5]

    @pl.when(other == 0)
    def _():
        slab[at, 0:1] = block[:, 0:1]


def coarse_rows(slab, wc_ref, spread_ref, moved, first, count):
    cast = [slab[a, 0:16].astype(BF).reshape(128, 256) for a in range(first, first + count + 2)]
    for n in range(count):
        tall = None
        for k in range(3):
            total = None
            for i in range(3):
                term = jnp.dot(cast[n + i], wc_ref[i, k], preferred_element_type=F32)
                total = term if total is None else total + term
            total = total.reshape(16, 8, 256)
            gap = jnp.zeros((16, 1, 256), F32)
            if k == 0:
                total = jnp.concatenate([gap, total[:, :-1]], axis=1)
            elif k == 2:
                total = jnp.concatenate([total[:, 1:], gap], axis=1)
            else:
                kept = total[:, :, 192:256]
            tall = total if tall is None else tall + total
        gap = jnp.zeros((1, 8, 64), F32)
        total = (
            jnp.concatenate([gap, tall[:-1, :, 0:64]], axis=0)
            + tall[:, :, 64:128]
            + jnp.concatenate([tall[1:, :, 128:192], gap], axis=0)
        )
        moved[128 * n : 128 * n + 128, 0:64] = (kept + leaky_relu(total)).reshape(128, 64)
    total = None
    for h in range(8):
        rows = moved[pl.ds(h, 16 * count, stride=8), :].astype(BF)
        term = jnp.dot(rows[:, 0:64], spread_ref[h], preferred_element_type=F32)
        total = term if total is None else total + term
    return total.astype(BF)


def coarse_kernel_body(
    own_ref, near_ref, halo_ref, far_ref, far_halo_ref, last_ref, wc_ref, spread_ref, out_ref, slab, moved,
):
    band = lax.axis_index("blk")
    blocks = (
        (0, 2, own_ref[...]), (0, 0, halo_ref[...]), (1, 2, near_ref[...]), (1, 0, last_ref[0:80]),
        (2, 2, far_ref[...]), (2, 0, far_halo_ref[...]), (3, 2, last_ref[80:240]), (3, 0, last_ref[240:320]),
    )
    for place, first, block in blocks:
        lay(slab, first, jnp.bitwise_xor(band, place), block)
    out_ref[...] = coarse_rows(slab, wc_ref, spread_ref, moved, 0, 4).reshape(4, 16, 512)


def moved_by(x, sectors, band_of):
    count, bands = lax.axis_size("sector"), lax.axis_size("blk")
    pairs = []
    for s in range(count):
        for b in range(bands):
            if 0 <= band_of(b) < bands:
                pairs.append((s * bands + b, (s + sectors) % count * bands + band_of(b)))
    return lax.ppermute(x, ("sector", "blk"), pairs)


def shaped(*dims, dtype=BF):
    return jax.ShapeDtypeStruct(dims, dtype)


def run(kernel, outs, scratch, flops, name, *args, limit=24, hbm=(), aliases=None):
    return pl.pallas_call(
        kernel,
        out_shape=outs,
        in_specs=[pl.BlockSpec(memory_space=pltpu.HBM) if n in hbm else VMEM for n in range(len(args))],
        out_specs=jax.tree.map(lambda _: VMEM, outs),
        scratch_shapes=scratch,
        input_output_aliases=aliases or {},
        compiler_params=pltpu.CompilerParams(vmem_limit_bytes=limit << 20),
        cost_estimate=pl.CostEstimate(flops=flops, bytes_accessed=min(flops, 1 << 20), transcendentals=0),
        name=name,
    )(*args)


def per_device(features, residual_first, residual_second, shortcut_first, shortcut_second,
               first_reduce_weight, second_reduce_weight, coarse_kernel):
    sector_edge, corner = run(
        sector_edge_kernel, (shaped(ROWS, 16, 16, 128), shaped(ROWS, EDGE, 16, 128)), (), 2 << 30, "sector_edge", features[0:ROWS]
    )
    band_edge = run(band_edge_kernel, shaped(16, EDGE, 16, 128), (), 4 << 30, "band_edge", features[:, 0:8], corner)
    sector_edge = moved_by(sector_edge, -1, lambda b: b)
    band_edge = moved_by(band_edge, 0, lambda b: b - 1)
    corner = moved_by(corner, -1, lambda b: b - 1)
    held = (
        shaped(22, 22, 16, 256), shaped(21, 22, 16, 256), shaped(22, 20, 16, 256), shaped(21, 21, 16, 256),
        shaped(9, 11, 16, 128, dtype=F32),
    )
    made = run(
        inner_kernel,
        (shaped(4, 256, 256),) * 4 + (shaped(256, 512), shaped(256, 256), shaped(256, 256), shaped(256, 128)) + held,
        (
            pltpu.VMEM((14, 14, 16, 128), F32),
        ),
        1 << 20, "inner", features,
        residual_first, residual_second, shortcut_first, shortcut_second, first_reduce_weight,
    )
    weights, levels = made[:8], made[8:]
    levels = run(
        rows_kernel, held, (pltpu.VMEM((2, 14, 16, 128), F32),),
        1 << 20, "rows", *levels, sector_edge, *weights,
        aliases={n: n for n in range(5)},
    )
    *levels, band_edge, corner = lax.optimization_barrier((*levels, band_edge, corner))
    y, *_ = run(
        columns_kernel,
        (shaped(160, 256),) + held,
        (pltpu.VMEM((10, 6, 16, 128), F32), pltpu.VMEM((9, 11, 8, 384), F32)),
        4 << 30, "columns", *levels, band_edge, corner, *weights, second_reduce_weight,
        aliases={n: n + 1 for n in range(5)},
    )
    halo = moved_by(y[80:160], 1, lambda b: b)
    far_halo = moved_by(y[80:160], 1, lambda b: b ^ 2)
    far = moved_by(y, 0, lambda b: b ^ 2)
    near = moved_by(y, 0, lambda b: b ^ 1)
    wc, spread = run(
        late_kernel,
        (shaped(3, 3, 256, 256), shaped(8, 64, 512)),
        (), 4 << 30, "late", y, jnp.swapaxes(coarse_kernel, 3, 4), limit=8,
    )
    halo, far_halo, near, far, wc, spread = lax.optimization_barrier((halo, far_halo, near, far, wc, spread))
    last = moved_by(jnp.concatenate([halo, far, far_halo], axis=0), 0, lambda b: b ^ 1)
    return run(
        coarse_kernel_body,
        shaped(4, 16, 512),
        (pltpu.VMEM((6, 18, 8, 256), F32), pltpu.VMEM((512, 128), F32)),
        2 << 30, "coarse", y, near, halo, far, far_halo, last, wc, spread, limit=16,
    )


def solution(mesh):
    in_specs = (P("sector", "blk", None),) + (P(),) * 6 + (P(None, None, None, None, "blk"),)
    return jax.shard_map(
        per_device, mesh=mesh, in_specs=in_specs, out_specs=P("sector", None, "blk"), check_vma=False
    )
```

```python
import jax
import jax.numpy as jnp
from jax import lax
from jax.experimental import pallas as pl
from jax.experimental.pallas import tpu as pltpu
from jax.sharding import PartitionSpec as P

BF = jnp.bfloat16
F32 = jnp.float32
ROWS = 5
EDGE = 5
VMEM = pl.BlockSpec(memory_space=pltpu.VMEM)


def leaky_relu(values):
    return jnp.maximum(values, 0.01 * values)


def beside(tiles):
    gap = jnp.zeros(tiles.shape[:-2] + (1, tiles.shape[-1]), tiles.dtype)
    after = jnp.concatenate([tiles[..., 1:, :], gap], axis=-2)
    before = jnp.concatenate([gap, tiles[..., :-1, :]], axis=-2)
    lane = lax.broadcasted_iota(jnp.int32, tiles.shape, tiles.ndim - 1)
    return jnp.where(lane < 64, after, before)


def under(tiles):
    gap = jnp.zeros(tiles.shape[:-2] + (1, tiles.shape[-1]), tiles.dtype)
    return jnp.concatenate([gap, tiles[..., :-1, :]], axis=-2)


def put(ref, index, tiles, second=beside):
    ref[index + (slice(None), slice(0, 128))] = tiles
    ref[index + (slice(None), slice(128, 256))] = second(tiles)


def flat(tiles):
    return tiles.reshape(-1, tiles.shape[-1])


def spaced(ref, a, rows, a_step, r, cols, r_step):
    lines = []
    for n in range(rows):
        if r_step == 1:
            lines.append(ref[a + a_step * n, r : r + cols])
        else:
            lines.append(jnp.stack([ref[a + a_step * n, r + r_step * m] for m in range(cols)]))
    return jnp.stack(lines)


def pair_dot(source, weights):
    total = None
    for slot in range(4):
        term = jnp.dot(flat(source(slot)), weights[slot], preferred_element_type=F32)
        total = term if total is None else total + term
    return leaky_relu(total)


def along_a(source, weights, a, pairs, r, count):
    total = pair_dot(lambda s: spaced(source, a - 1 + s, pairs, 2, r, count, 1), weights)
    return total.reshape(pairs, count, 16, 256)


def along_r(source, weights, a, count, r, pairs):
    total = pair_dot(lambda s: spaced(source, a, count, 1, r + s, pairs, 2), weights)
    return total.reshape(count, pairs, 16, 256)


def fill_p(xx, pp, weights, a, pairs, r, count):
    for pair in range(pairs):
        for first in range(0, count, 8):
            width = min(8, count - first)
            total = along_a(xx, weights, a + 2 * pair, 1, r + 1 + first, width).astype(BF)[0]
            at = slice(r + 1 + first, r + 1 + first + width)
            for side in range(2):
                put(pp, (a + 2 * pair + side, at), total[:, :, 128 * side : 128 * side + 128])


def fill_q(xx, qq, weights, a, count, r, pairs, step):
    for first in range(a, a + count, step):
        rows = min(step, a + count - first)
        total = along_r(xx, weights, first, rows, r, pairs).astype(BF)
        for pair in range(pairs):
            for side in range(2):
                put(qq, (slice(first, first + rows), r + 2 * pair + side), total[:, pair, :, 128 * side : 128 * side + 128])


def fill_f(pp, qq, ff, part, wp, wq, a, a_pairs, r, r_pairs):
    count, span = 2 * a_pairs, 2 * r_pairs
    total = along_r(pp, wp, a, count, r, r_pairs)
    for pair in range(r_pairs):
        for side in range(2):
            part[0:count, 2 * pair + side] = total[:, pair, :, 128 * side : 128 * side + 128]
    total = along_a(qq, wq, a, a_pairs, r, span)
    for pair in range(a_pairs):
        for side in range(2):
            tiles = total[pair, :, :, 128 * side : 128 * side + 128] + part[2 * pair + side, 0:span]
            put(ff, (a + 2 * pair + side, slice(r + 1, r + 1 + span)), tiles.astype(BF), under)


def fill_g(ff, gg, w_oo, w_oe, w_eo, w_ee, a, rows, r, cols):
    def product(first_a, na, first_r, nr, weights):
        tiles = spaced(ff, first_a, na, 2, first_r + 1, nr, 2)
        total = jnp.dot(flat(tiles), weights[...], preferred_element_type=F32)
        return total.reshape(na, nr, 16, -1)

    odd = product(2 * a - 1, rows + 1, 2 * r - 1, cols + 1, w_oo)
    total = odd[:rows, :cols, :, 0:128] + odd[:rows, 1:, :, 128:256]
    total = total + (odd[1:, :cols, :, 256:384] + odd[1:, 1:, :, 384:512])
    mixed = product(2 * a - 1, rows + 1, 2 * r, cols, w_oe)
    total = total + (mixed[:rows, :, :, 0:128] + mixed[1:, :, :, 128:256])
    mixed = product(2 * a, rows, 2 * r - 1, cols + 1, w_eo)
    total = total + (mixed[:, :cols, :, 0:128] + mixed[:, 1:, :, 128:256])
    total = total + product(2 * a, rows, 2 * r, cols, w_ee)
    gg[a - 1 : a - 1 + rows, r + 1 : r + 1 + cols] = leaky_relu(total).astype(BF).astype(F32)


def sector_edge_kernel(x_ref, sector_ref, corner_ref):
    for a in range(ROWS):
        tiles = x_ref[a].reshape(x_ref.shape[1], 16, 128)
        sector_ref[a] = tiles
        corner_ref[a] = tiles[:EDGE]


def band_edge_kernel(x_ref, corner_ref, band_ref):
    band_ref[0:ROWS] = corner_ref[...]
    for a in range(ROWS, x_ref.shape[0]):
        band_ref[a] = x_ref[a].reshape(8, 16, 128)[:EDGE]


def inner_kernel(
    x_ref, wp_raw, wp2_raw, wq_raw, wq2_raw, w1_raw,
    wp, wp2, wq, wq2, w_oo, w_oe, w_eo, w_ee, xx, pp, qq, ff, gg,
    part,
):
    own = x_ref.shape[0]
    blank = jnp.zeros((1, 16, 256), BF)
    for a in range(own + ROWS):
        xx[a, 0:1] = blank
        pp[a, 0:1] = blank
        ff[a, 0:1] = blank
    for a in range(9):
        gg[a, 0:1] = jnp.zeros((1, 16, 128), F32)
    xx[own + ROWS] = jnp.zeros(xx.shape[1:], BF)
    qq[own + ROWS] = jnp.zeros(qq.shape[1:], BF)
    for a in range(own):
        put(xx, (a, slice(1, own + 1)), x_ref[a].reshape(own, 16, 128))

    zero = jnp.zeros((64, 64), BF)
    for raw, out in ((wp_raw, wp), (wq_raw, wq), (wp2_raw, wp2), (wq2_raw, wq2)):
        for slot in range(4):
            for block, height in enumerate((0, 1, 2, -1)):
                for side in range(2):
                    tap = slot - side
                    parts = []
                    for upper in range(2):
                        k = height - upper + 1
                        inside = 0 <= tap <= 2 and 0 <= k <= 2
                        parts.append(raw[tap, k] if inside else zero)
                    out[slot, 64 * block : 64 * block + 64, 128 * side : 128 * side + 128] = (
                        jnp.concatenate(parts, axis=1)
                    )
    taps = (
        (w_oo, ((0, 0), (0, 2), (2, 0), (2, 2))), (w_oe, ((0, 1), (2, 1))), (w_eo, ((1, 0), (1, 2))), (w_ee, ((1, 1),)),
    )
    for out, pairs in taps:
        for n, (i, j) in enumerate(pairs):
            at = slice(128 * n, 128 * n + 128)
            out[0:64, at] = w1_raw[i, j, 1]
            out[64:128, at] = w1_raw[i, j, 2]
            out[128:192, at] = jnp.zeros((64, 128), BF)
            out[192:256, at] = w1_raw[i, j, 0]

    fill_p(xx, pp, wp, 1, 7, 0, 16)
    fill_q(xx, qq, wq, 0, 16, 0, 7, 1)
    for pair in range(7):
        fill_f(pp, qq, ff, part, wp2, wq2, 1 + 2 * pair, 1, 0, 7)
    fill_g(ff, gg, w_oo, w_oe, w_eo, w_ee, 1, 6, 0, 7)


def rows_kernel(
    xx_in, pp_in, qq_in, ff_in, gg_in, sector_ref,
    wp, wp2, wq, wq2, w_oo, w_oe, w_eo, w_ee,
    xx, pp, qq, ff, gg, part,
):
    own = sector_ref.shape[1]
    for a in range(ROWS):
        put(xx, (own + a, slice(1, own + 1)), sector_ref[a])
    fill_p(xx, pp, wp, 15, 3, 0, 16)
    fill_q(xx, qq, wq, 16, 5, 0, 7, 1)
    for pair in range(3):
        fill_f(pp, qq, ff, part, wp2, wq2, 15 + 2 * pair, 1, 0, 7)
    fill_g(ff, gg, w_oo, w_oe, w_eo, w_ee, 7, 3, 0, 7)


def columns_kernel(
    xx_in, pp_in, qq_in, ff_in, gg_in, band_ref, corner_ref,
    wp, wp2, wq, wq2, w_oo, w_oe, w_eo, w_ee, w2_ref,
    y_ref, xx, pp, qq, ff, gg, part, cells,
):
    own = band_ref.shape[0]
    for a in range(own):
        put(xx, (a, slice(own + 1, own + 1 + EDGE)), band_ref[a])
    for a in range(ROWS):
        put(xx, (own + a, slice(own + 1, own + 1 + EDGE)), corner_ref[a])
    for first in (1, 11):
        total = along_a(xx, wp, first, 5, 17, EDGE).astype(BF)
        for pair in range(5):
            for side in range(2):
                tiles = total[pair, :, :, 128 * side : 128 * side + 128]
                put(pp, (first + 2 * pair + side, slice(17, 17 + EDGE)), tiles)
    fill_q(xx, qq, wq, 0, 21, 14, 3, 7)
    for first in (1, 11):
        fill_f(pp, qq, ff, part, wp2, wq2, first, 5, 14, 3)
    fill_g(ff, gg, w_oo, w_oe, w_eo, w_ee, 1, 9, 7, 3)

    even = gg[:, :, pl.ds(0, 8, stride=2), :]
    odd = gg[:, :, pl.ds(1, 8, stride=2), :]
    cells[:, :, :, 0:128] = even
    cells[:, :, :, 128:256] = odd
    cells[:, :, :, 256:384] = under(odd)
    total = None
    for i in range(3):
        for j in range(3):
            rows = flat(spaced(cells, i, 4, 2, j, 5, 2)).astype(BF)
            term = jnp.dot(rows[:, 0:256], w2_ref[i, j, 1:3].reshape(256, 256), preferred_element_type=F32)
            term = term + jnp.dot(rows[:, 256:384], w2_ref[i, j, 0], preferred_element_type=F32)
            total = term if total is None else total + term
    y_ref[...] = leaky_relu(total).astype(BF)


def late_kernel(y_ref, raw, coarse_out, spread_out):
    row = lax.broadcasted_iota(jnp.int32, (64, 512), 0)
    col = lax.broadcasted_iota(jnp.int32, (64, 512), 1)
    for h in range(8):
        spread_out[h] = jnp.where(col == row * 8 + h, 1.0, 0.0).astype(BF)
    band = lax.axis_index("blk")
    row = lax.broadcasted_iota(jnp.int32, (64, 256), 0)
    col = lax.broadcasted_iota(jnp.int32, (64, 256), 1)
    own = jnp.where(col == row + 64 * band, 1.0, 0.0).astype(BF)
    for i in range(3):
        for k in range(3):
            last = own if i == 1 and k == 1 else jnp.zeros((64, 256), BF)
            coarse_out[i, k] = jnp.concatenate([raw[i, 0, k], raw[i, 1, k], raw[i, 2, k], last], axis=0).T


def lay(slab, first, other, block):
    block = block.astype(F32).reshape(-1, 5, 8, 256)
    at = slice(first, first + block.shape[0])
    slab[at, pl.ds(4 * other + 1, 4)] = block[:, 1:5]

    @pl.when(other == 0)
    def _():
        slab[at, 0:1] = block[:, 0:1]


def coarse_rows(slab, wc_ref, spread_ref, moved, first, count):
    cast = [slab[a, 0:16].astype(BF).reshape(128, 256) for a in range(first, first + count + 2)]
    for n in range(count):
        tall = None
        for k in range(3):
            total = None
            for i in range(3):
                term = jnp.dot(cast[n + i], wc_ref[i, k], preferred_element_type=F32)
                total = term if total is None else total + term
            total = total.reshape(16, 8, 256)
            gap = jnp.zeros((16, 1, 256), F32)
            if k == 0:
                total = jnp.concatenate([gap, total[:, :-1]], axis=1)
            elif k == 2:
                total = jnp.concatenate([total[:, 1:], gap], axis=1)
            else:
                kept = total[:, :, 192:256]
            tall = total if tall is None else tall + total
        gap = jnp.zeros((1, 8, 64), F32)
        total = (
            jnp.concatenate([gap, tall[:-1, :, 0:64]], axis=0)
            + tall[:, :, 64:128]
            + jnp.concatenate([tall[1:, :, 128:192], gap], axis=0)
        )
        moved[128 * n : 128 * n + 128, 0:64] = (kept + leaky_relu(total)).reshape(128, 64)
    total = None
    for h in range(8):
        rows = moved[pl.ds(h, 16 * count, stride=8), :].astype(BF)
        term = jnp.dot(rows[:, 0:64], spread_ref[h], preferred_element_type=F32)
        total = term if total is None else total + term
    return total.astype(BF)


def coarse_kernel_body(own_ref, near_ref, far_ref, halo_ref, last_ref, wc_ref, spread_ref, out_ref, slab, moved):
    band = lax.axis_index("blk")
    odd = 2 * jnp.bitwise_and(band, 1)
    for place, block in enumerate((own_ref[...], near_ref[...], far_ref[...], last_ref[0:160])):
        lay(slab, 2, jnp.bitwise_xor(band, place), block)
    halves = (halo_ref[0:80], halo_ref[80:160], last_ref[240:320], last_ref[160:240])
    for place, block in enumerate(halves):
        lay(slab, 0, jnp.bitwise_xor(jnp.bitwise_xor(band, place), odd), block)
    out_ref[...] = coarse_rows(slab, wc_ref, spread_ref, moved, 0, 4).reshape(4, 16, 512)


def moved_by(x, sectors, band_of):
    count, bands = lax.axis_size("sector"), lax.axis_size("blk")
    pairs = []
    for s in range(count):
        for b in range(bands):
            if 0 <= band_of(b) < bands:
                pairs.append((s * bands + b, (s + sectors) % count * bands + band_of(b)))
    return lax.ppermute(x, ("sector", "blk"), pairs)


def shaped(*dims, dtype=BF):
    return jax.ShapeDtypeStruct(dims, dtype)


def run(kernel, outs, scratch, flops, name, *args, limit=24, hbm=(), aliases=None):
    return pl.pallas_call(
        kernel,
        out_shape=outs,
        in_specs=[pl.BlockSpec(memory_space=pltpu.HBM) if n in hbm else VMEM for n in range(len(args))],
        out_specs=jax.tree.map(lambda _: VMEM, outs),
        scratch_shapes=scratch,
        input_output_aliases=aliases or {},
        compiler_params=pltpu.CompilerParams(vmem_limit_bytes=limit << 20),
        cost_estimate=pl.CostEstimate(flops=flops, bytes_accessed=min(flops, 1 << 20), transcendentals=0),
        name=name,
    )(*args)


def per_device(features, residual_first, residual_second, shortcut_first, shortcut_second,
               first_reduce_weight, second_reduce_weight, coarse_kernel):
    sector_edge, corner = run(
        sector_edge_kernel, (shaped(ROWS, 16, 16, 128), shaped(ROWS, EDGE, 16, 128)), (), 2 << 30, "sector_edge", features[0:ROWS]
    )
    band_edge = run(band_edge_kernel, shaped(16, EDGE, 16, 128), (), 4 << 30, "band_edge", features[:, 0:8], corner)
    sector_edge = moved_by(sector_edge, -1, lambda b: b)
    band_edge = moved_by(band_edge, 0, lambda b: b - 1)
    corner = moved_by(corner, -1, lambda b: b - 1)
    held = (
        shaped(22, 22, 16, 256), shaped(21, 22, 16, 256), shaped(22, 20, 16, 256), shaped(21, 21, 16, 256),
        shaped(9, 11, 16, 128, dtype=F32),
    )
    made = run(
        inner_kernel,
        (shaped(4, 256, 256),) * 4 + (shaped(256, 512), shaped(256, 256), shaped(256, 256), shaped(256, 128)) + held,
        (
            pltpu.VMEM((14, 14, 16, 128), F32),
        ),
        1 << 20, "inner", features,
        residual_first, residual_second, shortcut_first, shortcut_second, first_reduce_weight,
    )
    weights, levels = made[:8], made[8:]
    levels = run(
        rows_kernel, held, (pltpu.VMEM((2, 14, 16, 128), F32),),
        1 << 20, "rows", *levels, sector_edge, *weights,
        aliases={n: n for n in range(5)},
    )
    *levels, band_edge, corner = lax.optimization_barrier((*levels, band_edge, corner))
    y, *_ = run(
        columns_kernel,
        (shaped(160, 256),) + held,
        (pltpu.VMEM((10, 6, 16, 128), F32), pltpu.VMEM((9, 11, 8, 384), F32)),
        4 << 30, "columns", *levels, band_edge, corner, *weights, second_reduce_weight,
        aliases={n: n + 1 for n in range(5)},
    )
    near = moved_by(y, 0, lambda b: b ^ 1)
    kept, both = lax.optimization_barrier((y, jnp.concatenate([y[80:160], near[80:160]], axis=0)))
    halo = moved_by(both, 1, lambda b: b ^ 2 if b % 2 else b)
    far = moved_by(kept, 0, lambda b: b ^ 2)
    wc, spread = run(
        late_kernel,
        (shaped(3, 3, 256, 256), shaped(8, 64, 512)),
        (), 4 << 30, "late", y, jnp.swapaxes(coarse_kernel, 3, 4), limit=8,
    )
    halo, far, wc, spread = lax.optimization_barrier((halo, far, wc, spread))
    last = moved_by(jnp.concatenate([far, halo], axis=0), 0, lambda b: b ^ 1)
    return run(
        coarse_kernel_body,
        shaped(4, 16, 512),
        (pltpu.VMEM((6, 18, 8, 256), F32), pltpu.VMEM((512, 128), F32)),
        2 << 30, "coarse", y, near, far, halo, last, wc, spread, limit=16,
    )


def solution(mesh):
    in_specs = (P("sector", "blk", None),) + (P(),) * 6 + (P(None, None, None, None, "blk"),)
    return jax.shard_map(
        per_device, mesh=mesh, in_specs=in_specs, out_specs=P("sector", None, "blk"), check_vma=False
    )
```
